1024 devices in a mesh: replica: 128 (over x, y_lo, z), fsdp: 8 (over y_hi, core).
Axes of the slice: x: 4, y: 8 (y_hi: 4, y_lo: 2; y = y_hi * 2 + y_lo), z: 16, core: 2. Of those that a mesh axis runs over, the one named last changes fastest.
Arguments:
- activations: bfloat16 [128, 1152, 5120], P('replica', 'fsdp'), may hold values from -6 to 6
- cotangent: bfloat16 [128, 1152, 512], P('replica', 'fsdp'), may hold values from -0.17675781 to 0.17675781
- momentum: float32 [128, 5120, 512], P('replica', 'fsdp'), may hold values from -6 to 6
Outputs:
- momentum_next: bfloat16 [128, 5120, 512], P('replica', 'fsdp')
- update: float32 [5120, 512], P('fsdp')
The draws below stay inside these ranges and needn't reach their ends.
All inputs are finite; a program needn't handle non-finite values.
Results may differ from the reference program's by a relative error of at most 0.015.
Values may be sent and summed in bfloat16 or wider, within the bound.
A program may use at most 32 MiB of HBM per device.

```python
import jax
import jax.numpy as jnp
from jax import lax

D = 5120
COLS = 512
TOK_DEV = 144
SPAN = 64
BAND = 8
TOKENS = 1152
REPLICAS = 128
N_REPLICA = 128
N_FSDP = 8


def block_levels(rng, shape, split, low, high):
    def one(position, parts):
        heights = jax.random.uniform(jax.random.fold_in(jax.random.fold_in(rng, 6), position), (parts,), jnp.float32, low / len(split), high / len(split))
        return jnp.repeat(jnp.exp(heights), shape[position] // parts).reshape((-1,) + (1,) * (len(shape) - position - 1))

    loudness = one(*split[0])
    for cut in split[1:]:
        loudness = loudness * one(*cut)
    return loudness


def noise(rng, extent, scale, bound, pieces=(), held_as=jnp.bfloat16):
    result = jax.random.normal(rng, extent, jnp.float32) * scale
    if len(pieces) > 0:
        result = block_levels(rng, extent, pieces, -0.22, 0.18) * result
    return jnp.clip(result, min=-bound, max=bound).astype(held_as)


def setup_inputs(seed: int = 0) -> dict:
    keys = jax.random.split(jax.random.key(seed), 4)
    return {
        "activations": noise(keys[0], (REPLICAS, TOKENS, D), 1.0, 6.0, ((0, 128), (1, 8))),
        "cotangent": noise(keys[1], (REPLICAS, TOKENS, COLS), (1.0 / TOKENS ** 0.5), 0.17675781, ((0, 128), (1, 8))),
        "momentum": noise(keys[2], (REPLICAS, D, COLS), 1.0, 6.0, ((0, 128), (1, 8)), jnp.float32),
    }


momentum_decay = 0.9
norm_eps = 1e-06

def dct_basis():
    freq = jnp.arange(BAND).astype(jnp.float32)[:, None]
    place = jnp.arange(SPAN).astype(jnp.float32)[None, :]
    factor = jnp.where(freq == 0.0, jnp.sqrt(1.0 / SPAN), jnp.sqrt(2.0 / SPAN)).astype(jnp.float32)
    return (factor * jnp.cos(jnp.pi * (2.0 * place + 1.0) * freq / (2.0 * SPAN))).astype(jnp.float32)

def band_of(matrix, basis):
    blocks = matrix.reshape(matrix.shape[0] // SPAN, SPAN, matrix.shape[1] // SPAN, SPAN)
    return jnp.einsum('kp,ipjq,lq->ijkl', basis, blocks, basis, precision=lax.Precision.HIGHEST)

def expand_band(coeffs, basis):
    blocks = jnp.einsum('kp,ijkl,lq->ipjq', basis, coeffs, basis, precision=lax.Precision.HIGHEST)
    return blocks.reshape(coeffs.shape[0] * SPAN, coeffs.shape[1] * SPAN)

def reference(activations, cotangent, momentum):
    dct_table = dct_basis()

    def one_replica(inputs):
        act_rows, cot_rows, mom_rows = inputs
        act_split = act_rows.reshape(N_FSDP, TOK_DEV, D).astype(jnp.float32)
        cot_split = cot_rows.reshape(N_FSDP, TOK_DEV, COLS).astype(jnp.float32)
        partial_value = jnp.einsum('stf,stc->sfc', act_split, cot_split).astype(jnp.bfloat16)
        partial_value = lax.optimization_barrier(partial_value)
        gradient = lax.optimization_barrier(jnp.sum(partial_value.astype(jnp.float32), axis=0))
        current = momentum_decay * mom_rows + gradient
        own_band = band_of(current, dct_table)
        remaining = (current - expand_band(own_band, dct_table)).astype(jnp.bfloat16)
        return (own_band, remaining)
    bands, momentum_next = lax.map(one_replica, (activations, cotangent, momentum))
    shared = lax.optimization_barrier(jnp.sum(bands, axis=0)) / N_REPLICA
    decoded = expand_band(shared, dct_table)
    blocks = decoded.reshape(D // SPAN, SPAN, COLS // SPAN, SPAN)
    scale_rms = jnp.sqrt(lax.optimization_barrier(jnp.mean(blocks * blocks, axis=(1, 3), keepdims=True)) + norm_eps)
    update = (blocks / scale_rms).reshape(D, COLS)
    return (momentum_next, update)
```

```python
import functools

import jax
import jax.numpy as jnp
import numpy as np
from jax import lax
from jax.experimental import pallas as pl
from jax.experimental.pallas import tpu as pltpu
from jax.sharding import PartitionSpec as P

MESH = pl.DeviceIdType.MESH
SPAN = 64
BAND = 8
DECAY = 0.9
EPS = 1e-06

T = 144
ROWS = 640
COLS = 512
NX, NYL, NZ, NH = 4, 2, 16, 4
N_REPLICA = NX * NYL * NZ
CHUNK = 128
NCHUNK = ROWS // CHUNK
TILES = 5
OWNER_STEP = 3
HIGH = lax.Precision.HIGHEST


def basis_table():
    freq = np.arange(BAND)[:, None]
    place = np.arange(SPAN)[None, :]
    scale = np.where(freq == 0, np.sqrt(1.0 / SPAN), np.sqrt(2.0 / SPAN))
    basis = scale * np.cos(np.pi * (2.0 * place + 1.0) * freq / (2.0 * SPAN))
    table = np.zeros((ROWS, 128), np.float64)
    for i in range(ROWS // SPAN):
        table[i * SPAN : (i + 1) * SPAN, i * BAND : (i + 1) * BAND] = basis.T
    return table.astype(np.float32)


def two_terms(table):
    high = table.astype(jnp.bfloat16)
    low = (table - high.astype(np.float32)).astype(jnp.bfloat16)
    return np.concatenate([high, low], axis=1)


def dot(a, b, ca, cb, precision=None):
    return lax.dot_general(
        a, b, (((ca,), (cb,)), ((), ())), preferred_element_type=jnp.float32, precision=precision
    )


def kernel(
    act, cot, mom, table, table2,
    out_next, out_update,
    act_v, buf_s, buf_g, cots, mom_v, tab, tab2, project, s_out, s_in, acc, next_v,
    vec, xbuf, corebuf, zbuf, ybuf, fin, update_v,
    load_sem, sem_s, sem_g, sem_c, send_sem, fwd_sem, s_send, s_recv, out_sem,
    x_send, x_recv, core_sem, z_send, z_recv, y_send, y_recv, f_send, f_recv, g_send, g_recv,
):
    rep = lax.axis_index("replica")
    f = lax.axis_index("fsdp")
    x = rep // (NYL * NZ)
    yl = lax.rem(rep // NZ, NYL)
    z = lax.rem(rep, NZ)
    h = f // 2
    c = lax.rem(f, 2)
    oc = 1 - c
    s = 1 - 2 * c

    def ring(v):
        return lax.rem(v + NH, NH)

    def dev(hh, cc, xx=None, yy=None, zz=None):
        xx = x if xx is None else xx
        yy = yl if yy is None else yy
        zz = z if zz is None else zz
        return {"replica": (xx * NYL + yy) * NZ + zz, "fsdp": hh * 2 + cc}

    def remote(src, dst, ss, rs, to):
        return pltpu.make_async_remote_copy(src, dst, ss, rs, device_id=to, device_id_type=MESH)

    def block(hh, cc):
        start = pl.multiple_of((hh * 2 + cc) * ROWS, ROWS)
        return act.at[0, :, pl.ds(start, ROWS)]

    loads = [
        pltpu.make_async_copy(act.at[0], act_v, load_sem.at[0]),
        pltpu.make_async_copy(cot.at[0], cots.at[2 + c], load_sem.at[1]),
        pltpu.make_async_copy(table2, tab2, load_sem.at[2]),
        pltpu.make_async_copy(table, tab, load_sem.at[3]),
        pltpu.make_async_copy(mom.at[0], mom_v, load_sem.at[4]),
        pltpu.make_async_copy(block(ring(h + s), c), buf_s.at[2 + c], load_sem.at[5]),
        pltpu.make_async_copy(block(h, c), buf_g.at[c], load_sem.at[6]),
    ]
    for copy in loads:
        copy.start()

    barrier = pltpu.get_barrier_semaphore()
    peers = [dev(h, c, xx=lax.rem(x + k, NX)) for k in range(1, NX)]
    peers += [dev(ring(h + k), c, yy=yy) for k in range(1, NH) for yy in range(NYL)]
    peers += [dev(h, c, yy=1 - yl)]
    peers += [dev(h, oc), dev(ring(h + 1), oc), dev(ring(h - 1), oc)]
    for peer in peers:
        pl.semaphore_signal(barrier, inc=1, device_id=peer, device_id_type=MESH)

    def greet(k, carry):
        pl.semaphore_signal(barrier, inc=1, device_id=dev(h, c, zz=lax.rem(z + k, NZ)), device_id_type=MESH)
        return carry

    lax.fori_loop(1, NZ, greet, 0)
    pl.semaphore_wait(barrier, len(peers) + NZ - 1)

    first = [
        remote(cot.at[0], cots.at[c], send_sem.at[0], sem_c.at[c], dev(ring(h + s), c)),
        remote(cot.at[0], cots.at[4 + c], send_sem.at[1], sem_c.at[4 + c], dev(ring(h - s), c)),
        remote(cot.at[0], cots.at[2 + c], send_sem.at[2], sem_c.at[2 + c], dev(h, oc)),
        remote(block(ring(h + s * -1), oc), buf_s.at[2 + c], send_sem.at[3], sem_s.at[2 + c], dev(h, oc)),
        remote(block(ring(h + 2), 0), buf_s.at[c], send_sem.at[4], sem_s.at[c], dev(ring(h + 1), 0)),
        remote(block(ring(h + 2), 1), buf_s.at[c], send_sem.at[5], sem_s.at[c], dev(ring(h - 1), 1)),
    ]
    second = [
        remote(block(h, oc), buf_g.at[c], send_sem.at[6], sem_g.at[c], dev(h, oc)),
        remote(block(ring(h - 1), 0), buf_g.at[2 + c], send_sem.at[7], sem_g.at[2 + c], dev(ring(h - 1), 0)),
        remote(block(ring(h + 1), 1), buf_g.at[2 + c], send_sem.at[8], sem_g.at[2 + c], dev(ring(h + 1), 1)),
    ]
    for copy in first:
        copy.start()

    for copy in loads[:3]:
        copy.wait()
    q = dot(cots[2 + c], tab2[0:COLS], 1, 0)
    q = q[:, :128] + q[:, 128:]

    def pack(band):
        return band[0:40] + pltpu.roll(band[40:80], 64, 1)

    def bands(d, carry):
        a = act_v[:, pl.ds(pl.multiple_of(d * ROWS, ROWS), ROWS)]
        p = dot(a, tab2[...], 1, 0)
        p = p[:, :128] + p[:, 128:]
        vec[d] = pack(dot(p, q, 0, 0, HIGH))
        return carry

    lax.fori_loop(0, 2 * NH, bands, 0)
    for copy in loads[3:5]:
        copy.wait()
    columns = tab[0:COLS]
    side = dot(DECAY * mom_v[...], columns, 1, 0, HIGH)
    vec[f] += pack(dot(tab[...], side, 0, 0, HIGH))

    x_copies = []
    for k in range(1, NX):
        to = lax.rem(x + k, NX)
        x_copies.append(
            remote(vec.at[pl.ds(2 * to, 2)], xbuf.at[k - 1], x_send.at[k - 1], x_recv.at[k - 1], dev(h, c, xx=to))
        )
    for copy in x_copies:
        copy.start()

    rows = tab[0:CHUNK]
    project[...] = dot(rows, rows, 1, 1, HIGH)

    def without_band(value):
        side = dot(value, tab[0:COLS], 1, 0, HIGH)
        side = dot(project[...], side, 1, 0, HIGH)
        return value - dot(side, tab[0:COLS], 1, 1, HIGH)

    forwards = [
        remote(cots.at[c], cots.at[4 + c], fwd_sem.at[0], sem_c.at[4 + c], dev(h, oc)),
        remote(cots.at[4 + c], cots.at[c], fwd_sem.at[1], sem_c.at[c], dev(h, oc)),
    ]
    first[0].wait_recv()
    forwards[0].start()
    first[1].wait_recv()
    forwards[1].start()
    first[0].wait_send()
    first[1].wait_send()
    for copy in second:
        copy.start()

    for copy in x_copies:
        copy.wait()
    vec[pl.ds(2 * x, 2)] = vec[pl.ds(2 * x, 2)] + (xbuf[0] + xbuf[1] + xbuf[2])

    core_copy = remote(vec.at[2 * x + oc], corebuf, core_sem.at[0], core_sem.at[1], dev(h, oc))
    core_copy.start()
    core_copy.wait()
    vec[2 * x + c] = vec[2 * x + c] + corebuf[...]

    mine = vec.at[2 * x + c]
    for t in range(TILES):
        owner = OWNER_STEP * t
        copy = remote(mine.at[pl.ds(8 * t, 8)], zbuf.at[z], z_send.at[t], z_recv, dev(h, c, zz=owner))

        @pl.when(z == owner)
        def _():
            zbuf[owner] = mine[pl.ds(8 * t, 8)]

        @pl.when(z != owner)
        def _():
            copy.start()

    loads[5].wait()
    remote(block(h, oc), buf_s.at[2 + oc], send_sem.at[3], sem_s.at[2 + oc], dev(h, oc)).wait_recv()
    for slot in range(2):
        remote(block(h, 0), buf_s.at[slot], send_sem.at[4], sem_s.at[slot], dev(h, oc)).wait_recv()
    remote(cot.at[0], cots.at[2 + oc], send_sem.at[2], sem_c.at[2 + oc], dev(h, oc)).wait_recv()
    remote(cot.at[0], cots.at[oc], send_sem.at[2], sem_c.at[oc], dev(h, oc)).wait_recv()
    remote(cot.at[0], cots.at[4 + oc], send_sem.at[2], sem_c.at[4 + oc], dev(h, oc)).wait_recv()

    def s_copy(k):
        at = pl.ds(pl.multiple_of(k * CHUNK, CHUNK), CHUNK)
        return remote(s_out.at[at], s_in.at[at], s_send.at[k], s_recv.at[k], dev(ring(h + s), c))

    def passed(k, carry):
        at = pl.ds(pl.multiple_of(k * CHUNK, CHUNK), CHUNK)
        a = buf_s[:, :, at].reshape(4 * T, CHUNK)
        g = dot(a, cots[0:4].reshape(4 * T, COLS), 0, 0)
        s_out[at] = without_band(g).astype(jnp.bfloat16)
        s_copy(k).start()
        return carry

    lax.fori_loop(0, NCHUNK, passed, 0)

    is_owner = jnp.logical_and(lax.rem(z, OWNER_STEP) == 0, z < OWNER_STEP * TILES)
    tile = z // OWNER_STEP

    for t in range(TILES):
        owner = OWNER_STEP * t

        @pl.when(z != owner)
        def _():
            remote(mine.at[pl.ds(8 * t, 8)], zbuf.at[z], z_send.at[t], z_recv, dev(h, c, zz=owner)).wait_send()

    def column_copy(yy):
        return remote(zbuf.at[NZ], ybuf.at[h * NYL + yl], y_send.at[yy], y_recv, dev(x, c, yy=yy))

    @pl.when(is_owner)
    def _():
        pltpu.make_async_copy(zbuf.at[pl.ds(0, NZ - 1)], zbuf.at[pl.ds(0, NZ - 1)], z_recv).wait()
        total = zbuf[0]
        for k in range(1, NZ):
            total = total + zbuf[k]
        zbuf[NZ] = total
        for yy in range(NYL):
            here = jnp.logical_and(h == x, yl == yy)

            @pl.when(here)
            def _():
                ybuf[h * NYL + yl] = total

            @pl.when(jnp.logical_not(here))
            def _():
                column_copy(yy).start()

        for yy in range(NYL):
            here = jnp.logical_and(h == x, yl == yy)

            @pl.when(jnp.logical_not(here))
            def _():
                column_copy(yy).wait_send()

    def spread(k):
        return remote(fin.at[tile], fin.at[tile], f_send.at[k], f_recv.at[tile], dev(h, c, zz=lax.rem(z + k, NZ)))

    @pl.when(jnp.logical_and(is_owner, h == x))
    def _():
        pltpu.make_async_copy(ybuf.at[pl.ds(0, 7)], ybuf.at[pl.ds(0, 7)], y_recv).wait()
        total = ybuf[0]
        for k in range(1, NH * NYL):
            total = total + ybuf[k]
        fin[tile] = total

        def go(k, carry):
            spread(k).start()
            return carry

        lax.fori_loop(1, NZ, go, 0)

        def end(k, carry):
            spread(k).wait_send()
            return carry

        lax.fori_loop(1, NZ, end, 0)

    def across(k):
        return remote(fin, fin, g_send.at[k - 1], g_recv, dev(h, c, xx=lax.rem(x + k, NX)))

    @pl.when(h == x)
    def _():
        for t in range(TILES):

            @pl.when(z != OWNER_STEP * t)
            def _():
                pltpu.make_async_copy(fin.at[t], fin.at[t], f_recv.at[t]).wait()

        for k in range(1, NX):
            across(k).start()
        for k in range(1, NX):
            across(k).wait_send()

    loads[6].wait()
    remote(block(h, oc), buf_g.at[oc], send_sem.at[6], sem_g.at[oc], dev(h, oc)).wait_recv()
    for slot in range(2, 4):
        remote(block(h, 0), buf_g.at[slot], send_sem.at[6], sem_g.at[slot], dev(h, oc)).wait_recv()

    def direct(k, carry):
        at = pl.ds(pl.multiple_of(k * CHUNK, CHUNK), CHUNK)
        a = buf_g[:, :, at].reshape(4 * T, CHUNK)
        g = dot(a, cots[2:6].reshape(4 * T, COLS), 0, 0)
        acc[at] = without_band(DECAY * mom_v[at] + g)
        return carry

    lax.fori_loop(0, NCHUNK, direct, 0)

    @pl.when(h != x)
    def _():
        pltpu.make_async_copy(fin, fin, g_recv).wait()

    total = fin[...].reshape(8 * TILES, 128) * (1.0 / N_REPLICA)
    low = lax.broadcasted_iota(jnp.int32, (8 * TILES, 128), 1) < 64
    upper = jnp.where(low, total, 0.0)
    lower = jnp.where(low, pltpu.roll(total, 64, 1), 0.0)
    shared = jnp.concatenate([upper, lower, jnp.zeros((48, 128), jnp.float32)], axis=0)
    row = lax.broadcasted_iota(jnp.int32, (128, 128), 0) // BAND
    col = lax.broadcasted_iota(jnp.int32, (128, 128), 1) // BAND
    same = (row == col).astype(jnp.float32)
    power = dot(dot(same, shared * shared, 1, 0, HIGH), same, 1, 0, HIGH) * (1.0 / (SPAN * SPAN))
    shared = shared / jnp.sqrt(power + EPS)
    wide = dot(shared, tab[0:COLS], 1, 1, HIGH)
    update_v[...] = dot(tab[...], wide, 1, 0, HIGH)
    update_copy = pltpu.make_async_copy(update_v, out_update, out_sem.at[NCHUNK])
    update_copy.start()

    def out_copy(k):
        at = pl.ds(pl.multiple_of(k * CHUNK, CHUNK), CHUNK)
        return pltpu.make_async_copy(next_v.at[at], out_next.at[0, at], out_sem.at[k])

    def finish(k, carry):
        at = pl.ds(pl.multiple_of(k * CHUNK, CHUNK), CHUNK)
        s_copy(k).wait_recv()
        next_v[at] = (acc[at] + s_in[at].astype(jnp.float32)).astype(jnp.bfloat16)
        out_copy(k).start()
        return carry

    lax.fori_loop(0, NCHUNK, finish, 0)

    def drain(k, carry):
        s_copy(k).wait_send()
        out_copy(k).wait()
        return carry

    lax.fori_loop(0, NCHUNK, drain, 0)
    update_copy.wait()
    for copy in first[2:] + second + forwards:
        copy.wait_send()


def solution(mesh):
    assert mesh.shape["replica"] == N_REPLICA and mesh.shape["fsdp"] == 2 * NH
    table = basis_table()
    table2 = two_terms(table)
    f32, b16, dma = jnp.float32, jnp.bfloat16, pltpu.SemaphoreType.DMA

    def local(activations, cotangent, momentum):
        return pl.pallas_call(
            kernel,
            out_shape=(
                jax.ShapeDtypeStruct((1, ROWS, COLS), b16),
                jax.ShapeDtypeStruct((ROWS, COLS), f32),
            ),
            in_specs=[pl.BlockSpec(memory_space=pl.ANY)] * 5,
            out_specs=(pl.BlockSpec(memory_space=pl.ANY),) * 2,
            scratch_shapes=[
                pltpu.VMEM((T, 2 * NH * ROWS), b16),
                pltpu.VMEM((4, T, ROWS), b16),
                pltpu.VMEM((4, T, ROWS), b16),
                pltpu.VMEM((6, T, COLS), b16),
                pltpu.VMEM((ROWS, COLS), f32),
                pltpu.VMEM((ROWS, 128), f32),
                pltpu.VMEM((ROWS, 256), b16),
                pltpu.VMEM((CHUNK, CHUNK), f32),
                pltpu.VMEM((ROWS, COLS), b16),
                pltpu.VMEM((ROWS, COLS), b16),
                pltpu.VMEM((ROWS, COLS), f32),
                pltpu.VMEM((ROWS, COLS), b16),
                pltpu.VMEM((2 * NH, 8 * TILES, 128), f32),
                pltpu.VMEM((NX - 1, 2, 8 * TILES, 128), f32),
                pltpu.VMEM((8 * TILES, 128), f32),
                pltpu.VMEM((NZ + 1, 8, 128), f32),
                pltpu.VMEM((NH * NYL, 8, 128), f32),
                pltpu.VMEM((TILES, 8, 128), f32),
                pltpu.VMEM((ROWS, COLS), f32),
                dma((7,)), dma((4,)), dma((4,)), dma((6,)), dma((9,)), dma((2,)),
                dma((NCHUNK,)), dma((NCHUNK,)), dma((NCHUNK + 1,)),
                dma((NX - 1,)), dma((NX - 1,)), dma((2,)),
                dma((TILES,)), dma, dma((NYL,)), dma,
                dma((NZ,)), dma((TILES,)), dma((NX - 1,)), dma,
            ],
            compiler_params=pltpu.CompilerParams(
                collective_id=0, has_side_effects=True, vmem_limit_bytes=48 * 1024 * 1024
            ),
            cost_estimate=pl.CostEstimate(flops=2_000_000_000, bytes_accessed=6_000_000, transcendentals=0),
        )(activations, cotangent, momentum, jnp.asarray(table), jnp.asarray(table2))

    in_specs = (P("replica", "fsdp", None),) * 3
    out_specs = (P("replica", "fsdp", None), P("fsdp", None))
    return jax.shard_map(local, mesh=mesh, in_specs=in_specs, out_specs=out_specs, check_vma=False)
```

```python
import functools

import jax
import jax.numpy as jnp
import numpy as np
from jax import lax
from jax.experimental import pallas as pl
from jax.experimental.pallas import tpu as pltpu
from jax.sharding import PartitionSpec as P

MESH = pl.DeviceIdType.MESH
SPAN = 64
BAND = 8
DECAY = 0.9
EPS = 1e-06

T = 144
ROWS = 640
COLS = 512
NX, NYL, NZ, NH = 4, 2, 16, 4
N_REPLICA = NX * NYL * NZ
CHUNK = 128
NCHUNK = ROWS // CHUNK
TILES = 5
OWNER = NZ - TILES
HIGH = lax.Precision.HIGHEST


def basis_table():
    freq = np.arange(BAND)[:, None]
    place = np.arange(SPAN)[None, :]
    scale = np.where(freq == 0, np.sqrt(1.0 / SPAN), np.sqrt(2.0 / SPAN))
    basis = scale * np.cos(np.pi * (2.0 * place + 1.0) * freq / (2.0 * SPAN))
    table = np.zeros((CHUNK, 128), np.float64)
    for i in range(CHUNK // SPAN):
        table[i * SPAN : (i + 1) * SPAN, i * BAND : (i + 1) * BAND] = basis.T
    return table.astype(np.float32)


def split(value):
    high = value.astype(jnp.bfloat16)
    return high, (value - high.astype(jnp.float32)).astype(jnp.bfloat16)


def turn(value, by):
    return value if by == 0 else pltpu.roll(value, by, 1)


def dot(a, b, ca, cb, precision=None):
    return lax.dot_general(
        a, b, (((ca,), (cb,)), ((), ())), preferred_element_type=jnp.float32, precision=precision
    )


def kernel(
    act, cot, mom, table,
    out_next, out_bands,
    act_v, buf_s, buf_g, cots, mom_v, tab, tab2, project, side_v, p_v, s_out, s_in, acc, next_v,
    vec, xbuf, corebuf, zbuf, ybuf, fin,
    go_sem, far_sem, load_sem, sem_s, sem_g, sem_c, send_sem, fwd_sem, s_send, s_recv, out_sem,
    x_send, x_recv, core_sem, z_send, z_recv, y_send, y_recv, f_send, f_recv, g_send, g_recv,
):
    rep = lax.axis_index("replica")
    f = lax.axis_index("fsdp")
    x = rep // (NYL * NZ)
    yl = lax.rem(rep // NZ, NYL)
    z = lax.rem(rep, NZ)
    h = f // 2
    c = lax.rem(f, 2)
    oc = 1 - c
    s = 1 - 2 * c

    def ring(v):
        return lax.rem(v + NH, NH)

    def dev(hh, cc, xx=None, yy=None, zz=None):
        xx = x if xx is None else xx
        yy = yl if yy is None else yy
        zz = z if zz is None else zz
        return {"replica": (xx * NYL + yy) * NZ + zz, "fsdp": hh * 2 + cc}

    def remote(src, dst, ss, rs, to):
        return pltpu.make_async_remote_copy(src, dst, ss, rs, device_id=to, device_id_type=MESH)

    def block(hh, cc):
        start = pl.multiple_of((hh * 2 + cc) * ROWS, ROWS)
        return act.at[0, :, pl.ds(start, ROWS)]

    loads = [
        pltpu.make_async_copy(table, tab, load_sem.at[0]),
        pltpu.make_async_copy(cot.at[0], cots.at[2 + c], load_sem.at[1]),
        pltpu.make_async_copy(mom.at[0], mom_v, load_sem.at[2]),
        pltpu.make_async_copy(block(ring(h + s), c), buf_s.at[2 + c], load_sem.at[3]),
        pltpu.make_async_copy(block(h, c), buf_g.at[c], load_sem.at[4]),
    ]
    loads += [
        pltpu.make_async_copy(act.at[0, :, pl.ds(d * ROWS, ROWS)], act_v.at[d], load_sem.at[5 + d])
        for d in range(2 * NH)
    ]
    for copy in loads:
        copy.start()

    barrier = pltpu.get_barrier_semaphore()
    first_one = f == 0

    @pl.when(jnp.logical_not(first_one))
    def _():
        pl.semaphore_signal(barrier, inc=1, device_id={"replica": rep, "fsdp": 0}, device_id_type=MESH)

    loads[0].wait()
    rows = tab[...]
    for k in range(NCHUNK):
        high, low = split(turn(rows, 2 * BAND * k))
        tab2[k * CHUNK : (k + 1) * CHUNK] = jnp.concatenate([high, low], axis=1)
    high, low = split(dot(rows, rows, 1, 1, HIGH))
    project[...] = jnp.concatenate([high, low], axis=1)

    @pl.when(first_one)
    def _():
        pl.semaphore_wait(barrier, 2 * NH - 1)
        for k in range(1, 2 * NH):
            pl.semaphore_signal(go_sem, inc=1, device_id={"replica": rep, "fsdp": k}, device_id_type=MESH)

    @pl.when(jnp.logical_not(first_one))
    def _():
        pl.semaphore_wait(go_sem, 1)

    first = [
        remote(cot.at[0], cots.at[c], send_sem.at[0], sem_c.at[c], dev(ring(h + s), c)),
        remote(cot.at[0], cots.at[4 + c], send_sem.at[1], sem_c.at[4 + c], dev(ring(h - s), c)),
        remote(cot.at[0], cots.at[2 + c], send_sem.at[2], sem_c.at[2 + c], dev(h, oc)),
        remote(block(ring(h + s * -1), oc), buf_s.at[2 + c], send_sem.at[3], sem_s.at[2 + c], dev(h, oc)),
        remote(block(ring(h + 2), 0), buf_s.at[c], send_sem.at[4], sem_s.at[c], dev(ring(h + 1), 0)),
        remote(block(ring(h + 2), 1), buf_s.at[c], send_sem.at[5], sem_s.at[c], dev(ring(h - 1), 1)),
    ]
    second = [
        remote(block(h, oc), buf_g.at[c], send_sem.at[6], sem_g.at[c], dev(h, oc)),
        remote(block(ring(h - 1), 0), buf_g.at[2 + c], send_sem.at[7], sem_g.at[2 + c], dev(ring(h - 1), 0)),
        remote(block(ring(h + 1), 1), buf_g.at[2 + c], send_sem.at[8], sem_g.at[2 + c], dev(ring(h + 1), 1)),
    ]
    for copy in first:
        copy.start()

    far = [dev(h, c, xx=lax.rem(x + k, NX)) for k in range(1, NX)]

    @pl.when(jnp.logical_not(first_one))
    def _():
        for peer in far:
            pl.semaphore_signal(barrier, inc=1, device_id=peer, device_id_type=MESH)
        for k in range(NH):

            @pl.when(k + c > 0)
            def _():
                pl.semaphore_signal(barrier, inc=1, device_id=dev(k, c, yy=1 - yl), device_id_type=MESH)

        def greet(k, carry):
            pl.semaphore_signal(barrier, inc=1, device_id=dev(h, c, zz=lax.rem(z + k, NZ)), device_id_type=MESH)
            return carry

        lax.fori_loop(1, NZ, greet, 0)

    for copy in loads[1:3] + loads[5:]:
        copy.wait()
    columns = tab2[0:COLS]

    def sides(value):
        high, low = split(value)
        wide = dot(high, columns, 1, 0)
        return wide[:, :128] + wide[:, 128:] + dot(low, columns[:, :128], 1, 0)

    def pack(band):
        return band[0:40] + pltpu.roll(band[40:80], 64, 1)

    q = dot(cots[2 + c], columns, 1, 0)
    q = q[:, :128] + q[:, 128:]
    q_high, q_low = split(q)
    q_both = (q_high.astype(jnp.float32) + pltpu.roll(q_low.astype(jnp.float32), 64, 1)).astype(jnp.bfloat16)
    q_all = jnp.concatenate([q_both, q_high], axis=0)
    p = dot(act_v[...].reshape(2 * NH * T, ROWS), tab2[...], 1, 0)
    p = p[:, :128] + p[:, 128:]
    for d in range(2 * NH):
        p_high, p_low = split(p[d * T : (d + 1) * T])
        p_v[0:T, d * 128 : (d + 1) * 128] = p_high
        p_v[T : 2 * T, d * 128 : (d + 1) * 128] = p_low
    bands = dot(q_all, p_v[...], 0, 0)
    bands = bands[0:64] + bands[64:128]
    for d in range(2 * NH):
        part = bands[:, d * 128 : (d + 1) * 128]
        vec[d] = pack(jnp.concatenate([part, jnp.zeros_like(part)], axis=0).T)
    side_v[...] = sides(DECAY * mom_v[...])
    side_high, side_low = split(side_v[...])
    own = dot(tab2[...], side_high, 0, 0)
    own = own[0:128] + own[128:256] + dot(tab2[:, :128], side_low, 0, 0)
    vec[f] += pack(own)

    forwards = [
        remote(cots.at[c], cots.at[4 + c], fwd_sem.at[0], sem_c.at[4 + c], dev(h, oc)),
        remote(cots.at[4 + c], cots.at[c], fwd_sem.at[1], sem_c.at[c], dev(h, oc)),
    ]
    first[0].wait_recv()
    forwards[0].start()
    first[1].wait_recv()
    forwards[1].start()
    first[0].wait_send()
    first[1].wait_send()
    for copy in second:
        copy.start()

    @pl.when(jnp.logical_not(first_one))
    def _():
        pl.semaphore_wait(barrier, len(far) + NZ - 1 + NH - 1 + c)

    @pl.when(f == 1)
    def _():
        pl.semaphore_signal(far_sem, inc=1, device_id={"replica": rep, "fsdp": 0}, device_id_type=MESH)

    @pl.when(first_one)
    def _():
        pl.semaphore_wait(far_sem, 1)

    is_owner = z >= OWNER
    tile = lax.rem(z + TILES, NZ)

    mine = vec.at[2 * x + c]

    def s_copy(k):
        at = pl.ds(pl.multiple_of(k * CHUNK, CHUNK), CHUNK)
        return remote(s_out.at[at], s_in.at[at], s_send.at[k], s_recv.at[k], dev(ring(h + s), c))

    def low_part(side):
        high, low = split(side)
        rows = []
        for k in range(NCHUNK):
            top = high[k * CHUNK : (k + 1) * CHUNK]
            both = jnp.concatenate([top, top], axis=0)
            rows.append(dot(project[...], both, 1, 0) + dot(project[:, :128], low[k * CHUNK : (k + 1) * CHUNK], 1, 0))
        high, low = split(jnp.concatenate(rows, axis=0))
        return dot(jnp.concatenate([high, high], axis=1), columns, 1, 1) + dot(low, columns[:, :128], 1, 1)

    def near_sums():
        x_copies = []
        for k in range(1, NX):
            to = lax.rem(x + k, NX)
            x_copies.append(
                remote(vec.at[pl.ds(2 * to, 2)], xbuf.at[k - 1], x_send.at[k - 1], x_recv.at[k - 1], dev(h, c, xx=to))
            )
        for copy in x_copies:
            copy.start()

        for copy in x_copies:
            copy.wait()
        vec[pl.ds(2 * x, 2)] = vec[pl.ds(2 * x, 2)] + (xbuf[0] + xbuf[1] + xbuf[2])

        core_copy = remote(vec.at[2 * x + oc], corebuf, core_sem.at[0], core_sem.at[1], dev(h, oc))
        core_copy.start()
        core_copy.wait()
        vec[2 * x + c] = vec[2 * x + c] + corebuf[...]

        for t in range(TILES):
            owner = OWNER + t
            copy = remote(mine.at[pl.ds(8 * t, 8)], zbuf.at[z], z_send.at[t], z_recv, dev(h, c, zz=owner))

            @pl.when(z == owner)
            def _():
                zbuf[owner] = mine[pl.ds(8 * t, 8)]

            @pl.when(z != owner)
            def _():
                copy.start()

    def passed_on():
        loads[3].wait()
        remote(block(h, oc), buf_s.at[2 + oc], send_sem.at[3], sem_s.at[2 + oc], dev(h, oc)).wait_recv()
        for slot in range(2):
            remote(block(h, 0), buf_s.at[slot], send_sem.at[4], sem_s.at[slot], dev(h, oc)).wait_recv()
        remote(cot.at[0], cots.at[2 + oc], send_sem.at[2], sem_c.at[2 + oc], dev(h, oc)).wait_recv()
        remote(cot.at[0], cots.at[oc], send_sem.at[2], sem_c.at[oc], dev(h, oc)).wait_recv()
        remote(cot.at[0], cots.at[4 + oc], send_sem.at[2], sem_c.at[4 + oc], dev(h, oc)).wait_recv()

        acc[...] = dot(buf_s[...].reshape(4 * T, ROWS), cots[0:4].reshape(4 * T, COLS), 0, 0)
        s_out[...] = (acc[...] - low_part(sides(acc[...]))).astype(jnp.bfloat16)
        for k in range(NCHUNK):
            s_copy(k).start()

    def owner_sums():
        for t in range(TILES):
            owner = OWNER + t

            @pl.when(z != owner)
            def _():
                remote(mine.at[pl.ds(8 * t, 8)], zbuf.at[z], z_send.at[t], z_recv, dev(h, c, zz=owner)).wait_send()

        def column_copy(yy):
            return remote(zbuf.at[NZ], ybuf.at[h * NYL + yl], y_send.at[yy], y_recv, dev(x, c, yy=yy))

        @pl.when(is_owner)
        def _():
            pltpu.make_async_copy(zbuf.at[pl.ds(0, NZ - 1)], zbuf.at[pl.ds(0, NZ - 1)], z_recv).wait()
            total = zbuf[0]
            for k in range(1, NZ):
                total = total + zbuf[k]
            zbuf[NZ] = total
            for yy in range(NYL):
                here = jnp.logical_and(h == x, yl == yy)

                @pl.when(here)
                def _():
                    ybuf[h * NYL + yl] = total

                @pl.when(jnp.logical_not(here))
                def _():
                    column_copy(yy).start()

            for yy in range(NYL):
                here = jnp.logical_and(h == x, yl == yy)

                @pl.when(jnp.logical_not(here))
                def _():
                    column_copy(yy).wait_send()

        def spread(k):
            return remote(fin.at[tile], fin.at[tile], f_send.at[k], f_recv.at[tile], dev(h, c, zz=lax.rem(z + k, NZ)))

        @pl.when(jnp.logical_and(is_owner, h == x))
        def _():
            pltpu.make_async_copy(ybuf.at[pl.ds(0, 7)], ybuf.at[pl.ds(0, 7)], y_recv).wait()
            total = ybuf[0]
            for k in range(1, NH * NYL):
                total = total + ybuf[k]
            fin[tile] = total

            def go(k, carry):
                spread(k).start()
                return carry

            lax.fori_loop(1, NZ, go, 0)

            def end(k, carry):
                spread(k).wait_send()
                return carry

            lax.fori_loop(1, NZ, end, 0)

    def across_sums():
        def across(k):
            return remote(fin, fin, g_send.at[k - 1], g_recv, dev(h, c, xx=lax.rem(x + k, NX)))

        @pl.when(h == x)
        def _():
            for t in range(TILES):

                @pl.when(z != OWNER + t)
                def _():
                    pltpu.make_async_copy(fin.at[t], fin.at[t], f_recv.at[t]).wait()

            for k in range(1, NX):
                across(k).start()
            for k in range(1, NX):
                across(k).wait_send()

    def direct():
        loads[4].wait()
        remote(block(h, oc), buf_g.at[oc], send_sem.at[6], sem_g.at[oc], dev(h, oc)).wait_recv()
        for slot in range(2, 4):
            remote(block(h, 0), buf_g.at[slot], send_sem.at[6], sem_g.at[slot], dev(h, oc)).wait_recv()

        acc[...] = dot(buf_g[...].reshape(4 * T, ROWS), cots[2:6].reshape(4 * T, COLS), 0, 0)
        acc[...] = DECAY * mom_v[...] + acc[...] - low_part(side_v[...] + sides(acc[...]))

    def bands_out():
        @pl.when(h != x)
        def _():
            pltpu.make_async_copy(fin, fin, g_recv).wait()

        bands_copy = pltpu.make_async_copy(fin, out_bands, out_sem.at[NCHUNK])
        bands_copy.start()
        bands_copy.wait()

    near_sums()
    passed_on()
    owner_sums()
    direct()
    across_sums()

    def out_copy(k):
        at = pl.ds(pl.multiple_of(k * CHUNK, CHUNK), CHUNK)
        return pltpu.make_async_copy(next_v.at[at], out_next.at[0, at], out_sem.at[k])

    def finish(k, carry):
        at = pl.ds(pl.multiple_of(k * CHUNK, CHUNK), CHUNK)
        s_copy(k).wait_recv()
        next_v[at] = (acc[at] + s_in[at].astype(jnp.float32)).astype(jnp.bfloat16)
        out_copy(k).start()
        return carry

    lax.fori_loop(0, NCHUNK, finish, 0)
    bands_out()

    def drain(k, carry):
        s_copy(k).wait_send()
        out_copy(k).wait()
        return carry

    lax.fori_loop(0, NCHUNK, drain, 0)
    for copy in first[2:] + second + forwards:
        copy.wait_send()


def close(bands, table, value, out_next, out_update, update_v, value_v, sem):
    held = pltpu.make_async_copy(value, value_v, sem.at[NCHUNK])
    held.start()
    total = bands[...].reshape(8 * TILES, 128) * (1.0 / N_REPLICA)
    left = lax.broadcasted_iota(jnp.int32, (8 * TILES, 128), 1) < 64
    upper = jnp.where(left, total, 0.0)
    lower = jnp.where(left, pltpu.roll(total, 64, 1), 0.0)
    shared = jnp.concatenate([upper, lower, jnp.zeros((48, 128), jnp.float32)], axis=0)
    row = lax.broadcasted_iota(jnp.int32, (128, 128), 0) // BAND
    col = lax.broadcasted_iota(jnp.int32, (128, 128), 1) // BAND
    same = (row == col).astype(jnp.float32)
    power = dot(dot(same, shared * shared, 1, 0, HIGH), same, 1, 0, HIGH) * (1.0 / (SPAN * SPAN))
    shared = shared / jnp.sqrt(power + EPS)
    held.wait()
    copy = pltpu.make_async_copy(value_v, out_next, sem.at[NCHUNK])
    copy.start()
    rows = table[...]
    columns = [split(turn(rows, 2 * BAND * k)) for k in range(COLS // CHUNK)]
    high, low = split(shared)
    left, right = jnp.concatenate([high, high], axis=1), low
    wide = [
        dot(left, jnp.concatenate([a, b], axis=1), 1, 1) + dot(right, a, 1, 1) for a, b in columns
    ]
    high, low = split(jnp.concatenate(wide, axis=1))
    below = jnp.concatenate([high, low], axis=0)
    copies = []
    for k in range(NCHUNK):
        at = pl.ds(k * CHUNK, CHUNK)
        a, b = split(turn(rows, 2 * BAND * k))
        update_v[at] = dot(jnp.concatenate([a, a], axis=1), below, 1, 0) + dot(b, high, 1, 0)
        copies.append(pltpu.make_async_copy(update_v.at[at], out_update.at[at], sem.at[k]))
        copies[-1].start()
    for each in copies:
        each.wait()
    copy.wait()


def solution(mesh):
    assert mesh.shape["replica"] == N_REPLICA and mesh.shape["fsdp"] == 2 * NH
    table = basis_table()
    f32, b16, dma = jnp.float32, jnp.bfloat16, pltpu.SemaphoreType.DMA

    def local(activations, cotangent, momentum):
        rows = jnp.asarray(table)
        value, bands = pl.pallas_call(
            kernel,
            out_shape=(
                jax.ShapeDtypeStruct((1, ROWS, COLS), b16),
                jax.ShapeDtypeStruct((TILES, 8, 128), f32),
            ),
            in_specs=[pl.BlockSpec(memory_space=pl.ANY)] * 4,
            out_specs=(pl.BlockSpec(memory_space=pl.ANY),) * 2,
            scratch_shapes=[
                pltpu.VMEM((2 * NH, T, ROWS), b16),
                pltpu.VMEM((4, T, ROWS), b16),
                pltpu.VMEM((4, T, ROWS), b16),
                pltpu.VMEM((6, T, COLS), b16),
                pltpu.VMEM((ROWS, COLS), f32),
                pltpu.VMEM((CHUNK, 128), f32),
                pltpu.VMEM((ROWS, 256), b16),
                pltpu.VMEM((CHUNK, 256), b16),
                pltpu.VMEM((ROWS, 128), f32),
                pltpu.VMEM((2 * T, 2 * NH * 128), b16),
                pltpu.VMEM((ROWS, COLS), b16),
                pltpu.VMEM((ROWS, COLS), b16),
                pltpu.VMEM((ROWS, COLS), f32),
                pltpu.VMEM((ROWS, COLS), b16),
                pltpu.VMEM((2 * NH, 8 * TILES, 128), f32),
                pltpu.VMEM((NX - 1, 2, 8 * TILES, 128), f32),
                pltpu.VMEM((8 * TILES, 128), f32),
                pltpu.VMEM((NZ + 1, 8, 128), f32),
                pltpu.VMEM((NH * NYL, 8, 128), f32),
                pltpu.VMEM((TILES, 8, 128), f32),
                pltpu.SemaphoreType.REGULAR, pltpu.SemaphoreType.REGULAR,
                dma((5 + 2 * NH,)), dma((4,)), dma((4,)), dma((6,)), dma((9,)), dma((2,)),
                dma((NCHUNK,)), dma((NCHUNK,)), dma((NCHUNK + 1,)),
                dma((NX - 1,)), dma((NX - 1,)), dma((2,)),
                dma((TILES,)), dma, dma((NYL,)), dma,
                dma((NZ,)), dma((TILES,)), dma((NX - 1,)), dma,
            ],
            compiler_params=pltpu.CompilerParams(
                collective_id=0, has_side_effects=True, vmem_limit_bytes=60 * 1024 * 1024
            ),
            cost_estimate=pl.CostEstimate(flops=2_000_000_000, bytes_accessed=6_000_000, transcendentals=0),
        )(activations, cotangent, momentum, rows)
        return pl.pallas_call(
            close,
            out_shape=(
                jax.ShapeDtypeStruct((1, ROWS, COLS), b16),
                jax.ShapeDtypeStruct((ROWS, COLS), f32),
            ),
            in_specs=[pl.BlockSpec(memory_space=pltpu.VMEM)] * 2 + [pl.BlockSpec(memory_space=pl.ANY)],
            out_specs=(pl.BlockSpec(memory_space=pl.ANY),) * 2,
            scratch_shapes=[pltpu.VMEM((ROWS, COLS), f32), pltpu.VMEM((1, ROWS, COLS), b16), dma((NCHUNK + 1,))],
            compiler_params=pltpu.CompilerParams(vmem_limit_bytes=60 * 1024 * 1024),
            cost_estimate=pl.CostEstimate(flops=500_000_000, bytes_accessed=4_000_000, transcendentals=0),
        )(bands, rows, value)

    in_specs = (P("replica", "fsdp", None),) * 3
    out_specs = (P("replica", "fsdp", None), P("fsdp", None))
    return jax.shard_map(local, mesh=mesh, in_specs=in_specs, out_specs=out_specs, check_vma=False)
```

```python
import functools

import jax
import jax.numpy as jnp
import numpy as np
from jax import lax
from jax.experimental import pallas as pl
from jax.experimental.pallas import tpu as pltpu
from jax.sharding import PartitionSpec as P

MESH = pl.DeviceIdType.MESH
SPAN = 64
BAND = 8
DECAY = 0.9
EPS = 1e-06

T = 144
ROWS = 640
COLS = 512
NX, NYL, NZ, NH = 4, 2, 16, 4
N_REPLICA = NX * NYL * NZ
CHUNK = 128
NCHUNK = ROWS // CHUNK
PIECES = 3
PACKED = 16 * PIECES
HIGH = lax.Precision.HIGHEST


def basis_table():
    freq = np.arange(BAND)[:, None]
    place = np.arange(SPAN)[None, :]
    scale = np.where(freq == 0, np.sqrt(1.0 / SPAN), np.sqrt(2.0 / SPAN))
    basis = scale * np.cos(np.pi * (2.0 * place + 1.0) * freq / (2.0 * SPAN))
    table = np.zeros((CHUNK, 128), np.float64)
    for i in range(CHUNK // SPAN):
        table[i * SPAN : (i + 1) * SPAN, i * BAND : (i + 1) * BAND] = basis.T
    return table.astype(np.float32)


def split(value):
    high = value.astype(jnp.bfloat16)
    return high, (value - high.astype(jnp.float32)).astype(jnp.bfloat16)


def turn(value, by):
    return value if by == 0 else pltpu.roll(value, by, 1)


def dot(a, b, ca, cb, precision=None):
    return lax.dot_general(
        a, b, (((ca,), (cb,)), ((), ())), preferred_element_type=jnp.float32, precision=precision
    )


def kernel(
    act, cot, mom, table,
    out_next, out_bands,
    act_v, buf_s, buf_g, cots, mom_v, tab, tab2, project, side_v, p_v, s_out, s_in, acc, next_v,
    vec, xbuf, mine, zbuf, ybuf, fin, fin_in,
    go_sem, column_sem, load_sem, sem_s, sem_g, sem_c, send_sem, fwd_sem, s_send, s_recv, out_sem,
    x_send, x_recv, z_send, z_recv, y_send, y_recv, f_send, f_recv,
):
    rep = lax.axis_index("replica")
    f = lax.axis_index("fsdp")
    x = rep // (NYL * NZ)
    yl = lax.rem(rep // NZ, NYL)
    z = lax.rem(rep, NZ)
    h = f // 2
    c = lax.rem(f, 2)
    oc = 1 - c
    s = 1 - 2 * c

    def ring(v):
        return lax.rem(v + NH, NH)

    def dev(hh, cc, xx=None, yy=None, zz=None):
        xx = x if xx is None else xx
        yy = yl if yy is None else yy
        zz = z if zz is None else zz
        return {"replica": (xx * NYL + yy) * NZ + zz, "fsdp": hh * 2 + cc}

    def remote(src, dst, ss, rs, to):
        return pltpu.make_async_remote_copy(src, dst, ss, rs, device_id=to, device_id_type=MESH)

    def block(hh, cc):
        start = pl.multiple_of((hh * 2 + cc) * ROWS, ROWS)
        return act.at[0, :, pl.ds(start, ROWS)]

    loads = [
        pltpu.make_async_copy(table, tab, load_sem.at[0]),
        pltpu.make_async_copy(cot.at[0], cots.at[2 + c], load_sem.at[1]),
        pltpu.make_async_copy(mom.at[0], mom_v, load_sem.at[2]),
        pltpu.make_async_copy(block(ring(h + s), c), buf_s.at[2 + c], load_sem.at[3]),
        pltpu.make_async_copy(block(h, c), buf_g.at[c], load_sem.at[4]),
    ]
    loads += [
        pltpu.make_async_copy(act.at[0, :, pl.ds(d * ROWS, ROWS)], act_v.at[d], load_sem.at[5 + d])
        for d in range(2 * NH)
    ]
    for copy in loads:
        copy.start()

    y = NYL * h + yl
    ny = NYL * NH
    place = lax.rem(y - NYL * x + ny, ny)

    def lead_at(where):
        where = lax.rem(where + 2 * ny, ny)
        return jnp.where(jnp.logical_and(where >= 1, where <= 5), 1, 0)

    lead_core = lead_at(place)
    leads = c == lead_core
    barrier = pltpu.get_barrier_semaphore()

    def signal(sem, to):
        pl.semaphore_signal(sem, inc=1, device_id=to, device_id_type=MESH)

    @pl.when(jnp.logical_not(leads))
    def _():
        signal(barrier, dev(h, lead_core))

    for k in (-1, 1):
        signal(barrier, dev(ring(h + k), lead_at(place + NYL * k)))
    for k in range(1, NX):
        xx = lax.rem(x + k, NX)
        signal(barrier, dev(h, lead_at(y - NYL * xx), xx=xx))

    loads[0].wait()
    rows = tab[...]
    for k in range(NCHUNK):
        high, low = split(turn(rows, 2 * BAND * k))
        tab2[k * CHUNK : (k + 1) * CHUNK] = jnp.concatenate([high, low], axis=1)
    high, low = split(dot(rows, rows, 1, 1, HIGH))
    project[...] = jnp.concatenate([high, low], axis=1)

    tells = jnp.logical_and(place == 4, c == 0)
    owns = jnp.logical_and(jnp.logical_not(leads), jnp.logical_or(place < 4, place > 5))
    piece = jnp.where(c == 0, place - 1, lax.rem(ny - place, ny))

    @pl.when(leads)
    def _():
        pl.semaphore_wait(barrier, 1 + 4 + 2 * (NX - 1))
        signal(go_sem, dev(h, 1 - lead_core))
        signal(barrier, dev(ring(x + 2), 0, yy=0))

    @pl.when(jnp.logical_not(leads))
    def _():
        pl.semaphore_wait(go_sem, 1)

    first = [
        remote(cot.at[0], cots.at[c], send_sem.at[0], sem_c.at[c], dev(ring(h + s), c)),
        remote(cot.at[0], cots.at[4 + c], send_sem.at[1], sem_c.at[4 + c], dev(ring(h - s), c)),
        remote(cot.at[0], cots.at[2 + c], send_sem.at[2], sem_c.at[2 + c], dev(h, oc)),
        remote(block(ring(h + s * -1), oc), buf_s.at[2 + c], send_sem.at[3], sem_s.at[2 + c], dev(h, oc)),
        remote(block(ring(h + 2), 0), buf_s.at[c], send_sem.at[4], sem_s.at[c], dev(ring(h + 1), 0)),
        remote(block(ring(h + 2), 1), buf_s.at[c], send_sem.at[5], sem_s.at[c], dev(ring(h - 1), 1)),
    ]
    second = [
        remote(block(h, oc), buf_g.at[c], send_sem.at[6], sem_g.at[c], dev(h, oc)),
        remote(block(ring(h - 1), 0), buf_g.at[2 + c], send_sem.at[7], sem_g.at[2 + c], dev(ring(h - 1), 0)),
        remote(block(ring(h + 1), 1), buf_g.at[2 + c], send_sem.at[8], sem_g.at[2 + c], dev(ring(h + 1), 1)),
    ]
    for copy in first[:4] + second[:1]:
        copy.start()

    @pl.when(owns)
    def _():
        def greet(k, carry):
            signal(barrier, dev(h, c, zz=lax.rem(z + k, NZ)))
            return carry

        lax.fori_loop(1, NZ, greet, 0)

    for copy in loads[1:3] + loads[5:]:
        copy.wait()
    columns = tab2[0:COLS]

    def sides(value):
        high, low = split(value)
        wide = dot(high, columns, 1, 0)
        return wide[:, :128] + wide[:, 128:] + dot(low, columns[:, :128], 1, 0)

    def pack(band):
        return jnp.concatenate([band[0:40] + pltpu.roll(band[40:80], 64, 1), jnp.zeros((8, 128), jnp.float32)], axis=0)

    q = dot(cots[2 + c], columns, 1, 0)
    q = q[:, :128] + q[:, 128:]
    q_high, q_low = split(q)
    q_both = (q_high.astype(jnp.float32) + pltpu.roll(q_low.astype(jnp.float32), 64, 1)).astype(jnp.bfloat16)
    q_all = jnp.concatenate([q_both, q_high], axis=0)
    p = dot(act_v[...].reshape(2 * NH * T, ROWS), tab2[...], 1, 0)
    p = p[:, :128] + p[:, 128:]
    for d in range(2 * NH):
        p_high, p_low = split(p[d * T : (d + 1) * T])
        p_v[0:T, d * 128 : (d + 1) * 128] = p_high
        p_v[T : 2 * T, d * 128 : (d + 1) * 128] = p_low
    bands = dot(q_all, p_v[...], 0, 0)
    bands = bands[0:64] + bands[64:128]
    for d in range(2 * NH):
        part = bands[:, d * 128 : (d + 1) * 128]
        vec[d] = pack(jnp.concatenate([part, jnp.zeros_like(part)], axis=0).T)
    side_v[...] = sides(DECAY * mom_v[...])
    side_high, side_low = split(side_v[...])
    own = dot(tab2[...], side_high, 0, 0)
    own = own[0:128] + own[128:256] + dot(tab2[:, :128], side_low, 0, 0)
    vec[f] += pack(own)

    forwards = [
        remote(cots.at[c], cots.at[4 + c], fwd_sem.at[0], sem_c.at[4 + c], dev(h, oc)),
        remote(cots.at[4 + c], cots.at[c], fwd_sem.at[1], sem_c.at[c], dev(h, oc)),
    ]

    def owner_y(xx, k):
        return lax.rem(NYL * xx + jnp.where(c == 0, 1 + k, ny - k), ny)

    def y_copy(k):
        yy = owner_y(x, k)
        return remote(mine.at[pl.ds(16 * k, 16)], ybuf.at[y], y_send.at[k], y_recv, dev(yy // NYL, c, yy=lax.rem(yy, NYL)))

    def z_copy(k):
        return remote(zbuf.at[z], zbuf.at[z], z_send.at[k], z_recv, dev(h, c, zz=lax.rem(z + k, NZ)))

    f_targets = []
    for xx in range(NX):
        for yy in range(NYL):
            here = jnp.logical_and(x == xx, jnp.logical_and(h == x, yl == yy))
            f_targets.append((xx * NYL + yy, dev(x, c, xx=xx, yy=yy), here))

    def f_copy(k, there):
        return remote(fin.at[piece], fin_in.at[piece], f_send.at[k], f_recv.at[piece], there)

    def s_copy(k):
        at = pl.ds(pl.multiple_of(k * CHUNK, CHUNK), CHUNK)
        return remote(s_out.at[at], s_in.at[at], s_send.at[k], s_recv.at[k], dev(ring(h + s), c))

    def low_part(side):
        high, low = split(side)
        rows = []
        for k in range(NCHUNK):
            top = high[k * CHUNK : (k + 1) * CHUNK]
            both = jnp.concatenate([top, top], axis=0)
            rows.append(dot(project[...], both, 1, 0) + dot(project[:, :128], low[k * CHUNK : (k + 1) * CHUNK], 1, 0))
        high, low = split(jnp.concatenate(rows, axis=0))
        return dot(jnp.concatenate([high, high], axis=1), columns, 1, 1) + dot(low, columns[:, :128], 1, 1)

    def plane_sums():
        copies = [remote(vec.at[2 * x + oc], xbuf.at[c], x_send.at[0], x_recv.at[c], dev(h, oc))]
        for k in range(1, NX):
            xx = lax.rem(x + k, NX)
            for m in range(2):
                copies.append(
                    remote(vec.at[2 * xx + m], xbuf.at[2 * k + c], x_send.at[2 * k + m], x_recv.at[2 * k + c], dev(h, m, xx=xx))
                )
        for copy in copies:
            copy.start()

        @pl.when(tells)
        def _():
            pl.semaphore_wait(barrier, ny)
            for k in range(ny):
                for m in range(2):
                    if (k, m) != (0, 0):
                        signal(column_sem, dev(ring(h + k // NYL), m, yy=k % NYL))

        def arrived(slot):
            pltpu.make_async_copy(xbuf.at[slot], xbuf.at[slot], x_recv.at[slot]).wait()

        arrived(oc)
        for slot in range(2, 2 * NX):
            arrived(slot)
        total = vec[2 * x + c] + xbuf[oc]
        for slot in range(2, 2 * NX):
            total = total + xbuf[slot]
        mine[...] = total

        @pl.when(jnp.logical_not(tells))
        def _():
            pl.semaphore_wait(column_sem, 1)

        for k in range(PIECES):
            copy = y_copy(k)
            here = owner_y(x, k) == y

            @pl.when(here)
            def _():
                ybuf[y] = mine[pl.ds(16 * k, 16)]

            @pl.when(jnp.logical_not(here))
            def _():
                copy.start()

        for copy in copies:
            copy.wait_send()

    def depth_sums():
        @pl.when(owns)
        def _():
            pl.semaphore_wait(barrier, NZ - 1)
            pltpu.make_async_copy(ybuf.at[pl.ds(0, ny - 1)], ybuf.at[pl.ds(0, ny - 1)], y_recv).wait()
            total = ybuf[0]
            for k in range(1, ny):
                total = total + ybuf[k]
            zbuf[z] = total

            def go(k, carry):
                z_copy(k).start()
                return carry

            lax.fori_loop(1, NZ, go, 0)

    def passed_on():
        loads[3].wait()
        remote(block(h, oc), buf_s.at[2 + oc], send_sem.at[3], sem_s.at[2 + oc], dev(h, oc)).wait_recv()
        for slot in range(2):
            remote(block(h, 0), buf_s.at[slot], send_sem.at[4], sem_s.at[slot], dev(h, oc)).wait_recv()
        remote(cot.at[0], cots.at[2 + oc], send_sem.at[2], sem_c.at[2 + oc], dev(h, oc)).wait_recv()
        remote(cot.at[0], cots.at[oc], send_sem.at[2], sem_c.at[oc], dev(h, oc)).wait_recv()
        remote(cot.at[0], cots.at[4 + oc], send_sem.at[2], sem_c.at[4 + oc], dev(h, oc)).wait_recv()

        acc[...] = dot(buf_s[...].reshape(4 * T, ROWS), cots[0:4].reshape(4 * T, COLS), 0, 0)
        s_out[...] = (acc[...] - low_part(sides(acc[...]))).astype(jnp.bfloat16)
        for k in range(NCHUNK):
            s_copy(k).start()

    def spread_sums():
        for k in range(PIECES):

            @pl.when(owner_y(x, k) != y)
            def _():
                y_copy(k).wait_send()

        @pl.when(owns)
        def _():
            pltpu.make_async_copy(zbuf.at[pl.ds(0, NZ - 1)], zbuf.at[pl.ds(0, NZ - 1)], z_recv).wait()
            total = zbuf[0]
            for k in range(1, NZ):
                total = total + zbuf[k]
            fin[piece] = total
            for k, there, here in f_targets:
                copy = f_copy(k, there)

                @pl.when(jnp.logical_not(here))
                def _():
                    copy.start()

            def end(k, carry):
                z_copy(k).wait_send()
                return carry

            lax.fori_loop(1, NZ, end, 0)
            for k, there, here in f_targets:
                copy = f_copy(k, there)

                @pl.when(jnp.logical_not(here))
                def _():
                    copy.wait_send()

    def direct():
        loads[4].wait()
        remote(block(h, oc), buf_g.at[oc], send_sem.at[6], sem_g.at[oc], dev(h, oc)).wait_recv()
        for slot in range(2, 4):
            remote(block(h, 0), buf_g.at[slot], send_sem.at[6], sem_g.at[slot], dev(h, oc)).wait_recv()

        acc[...] = dot(buf_g[...].reshape(4 * T, ROWS), cots[2:6].reshape(4 * T, COLS), 0, 0)
        acc[...] = DECAY * mom_v[...] + acc[...] - low_part(side_v[...] + sides(acc[...]))

    def bands_out():
        for k in range(PIECES):
            here = jnp.logical_and(h == x, owner_y(h, k) == y)

            @pl.when(jnp.logical_not(here))
            def _():
                pltpu.make_async_copy(fin_in.at[k], fin_in.at[k], f_recv.at[k]).wait()

            @pl.when(here)
            def _():
                fin_in[k] = fin[k]

        bands_copy = pltpu.make_async_copy(fin_in, out_bands, out_sem.at[NCHUNK])
        bands_copy.start()
        bands_copy.wait()

    plane_sums()
    for copy in first[4:] + second[1:]:
        copy.start()
    first[0].wait_recv()
    forwards[0].start()
    first[1].wait_recv()
    forwards[1].start()
    depth_sums()
    passed_on()
    spread_sums()
    direct()

    def out_copy(k):
        at = pl.ds(pl.multiple_of(k * CHUNK, CHUNK), CHUNK)
        return pltpu.make_async_copy(next_v.at[at], out_next.at[0, at], out_sem.at[k])

    def finish(k, carry):
        at = pl.ds(pl.multiple_of(k * CHUNK, CHUNK), CHUNK)
        s_copy(k).wait_recv()
        next_v[at] = (acc[at] + s_in[at].astype(jnp.float32)).astype(jnp.bfloat16)
        out_copy(k).start()
        return carry

    lax.fori_loop(0, NCHUNK, finish, 0)
    bands_out()

    def drain(k, carry):
        s_copy(k).wait_send()
        out_copy(k).wait()
        return carry

    lax.fori_loop(0, NCHUNK, drain, 0)
    for copy in first + second + forwards:
        copy.wait_send()


def close(bands, table, value, out_next, out_update, update_v, value_v, sem):
    held = pltpu.make_async_copy(value, value_v, sem.at[NCHUNK])
    held.start()
    total = bands[...].reshape(PACKED, 128)[0:40] * (1.0 / N_REPLICA)
    left = lax.broadcasted_iota(jnp.int32, (40, 128), 1) < 64
    upper = jnp.where(left, total, 0.0)
    lower = jnp.where(left, pltpu.roll(total, 64, 1), 0.0)
    shared = jnp.concatenate([upper, lower, jnp.zeros((48, 128), jnp.float32)], axis=0)
    row = lax.broadcasted_iota(jnp.int32, (128, 128), 0) // BAND
    col = lax.broadcasted_iota(jnp.int32, (128, 128), 1) // BAND
    same = (row == col).astype(jnp.float32)
    power = dot(dot(same, shared * shared, 1, 0, HIGH), same, 1, 0, HIGH) * (1.0 / (SPAN * SPAN))
    shared = shared / jnp.sqrt(power + EPS)
    held.wait()
    copy = pltpu.make_async_copy(value_v, out_next, sem.at[NCHUNK])
    copy.start()
    rows = table[...]
    columns = [split(turn(rows, 2 * BAND * k)) for k in range(COLS // CHUNK)]
    high, low = split(shared)
    left, right = jnp.concatenate([high, high], axis=1), low
    wide = [
        dot(left, jnp.concatenate([a, b], axis=1), 1, 1) + dot(right, a, 1, 1) for a, b in columns
    ]
    high, low = split(jnp.concatenate(wide, axis=1))
    below = jnp.concatenate([high, low], axis=0)
    copies = []
    for k in range(NCHUNK):
        at = pl.ds(k * CHUNK, CHUNK)
        a, b = split(turn(rows, 2 * BAND * k))
        update_v[at] = dot(jnp.concatenate([a, a], axis=1), below, 1, 0) + dot(b, high, 1, 0)
        copies.append(pltpu.make_async_copy(update_v.at[at], out_update.at[at], sem.at[k]))
        copies[-1].start()
    for each in copies:
        each.wait()
    copy.wait()


def solution(mesh):
    assert mesh.shape["replica"] == N_REPLICA and mesh.shape["fsdp"] == 2 * NH
    table = basis_table()
    f32, b16, dma = jnp.float32, jnp.bfloat16, pltpu.SemaphoreType.DMA

    def local(activations, cotangent, momentum):
        rows = jnp.asarray(table)
        value, bands = pl.pallas_call(
            kernel,
            out_shape=(
                jax.ShapeDtypeStruct((1, ROWS, COLS), b16),
                jax.ShapeDtypeStruct((PIECES, 16, 128), f32),
            ),
            in_specs=[pl.BlockSpec(memory_space=pl.ANY)] * 4,
            out_specs=(pl.BlockSpec(memory_space=pl.ANY),) * 2,
            scratch_shapes=[
                pltpu.VMEM((2 * NH, T, ROWS), b16),
                pltpu.VMEM((4, T, ROWS), b16),
                pltpu.VMEM((4, T, ROWS), b16),
                pltpu.VMEM((6, T, COLS), b16),
                pltpu.VMEM((ROWS, COLS), f32),
                pltpu.VMEM((CHUNK, 128), f32),
                pltpu.VMEM((ROWS, 256), b16),
                pltpu.VMEM((CHUNK, 256), b16),
                pltpu.VMEM((ROWS, 128), f32),
                pltpu.VMEM((2 * T, 2 * NH * 128), b16),
                pltpu.VMEM((ROWS, COLS), b16),
                pltpu.VMEM((ROWS, COLS), b16),
                pltpu.VMEM((ROWS, COLS), f32),
                pltpu.VMEM((ROWS, COLS), b16),
                pltpu.VMEM((2 * NH, PACKED, 128), f32),
                pltpu.VMEM((2 * NX, PACKED, 128), f32),
                pltpu.VMEM((PACKED, 128), f32),
                pltpu.VMEM((NZ, 16, 128), f32),
                pltpu.VMEM((NH * NYL, 16, 128), f32),
                pltpu.VMEM((PIECES, 16, 128), f32),
                pltpu.VMEM((PIECES, 16, 128), f32),
                pltpu.SemaphoreType.REGULAR, pltpu.SemaphoreType.REGULAR,
                dma((5 + 2 * NH,)), dma((4,)), dma((4,)), dma((6,)), dma((9,)), dma((2,)),
                dma((NCHUNK,)), dma((NCHUNK,)), dma((NCHUNK + 1,)),
                dma((2 * NX,)), dma((2 * NX,)),
                dma((NZ,)), dma, dma((PIECES,)), dma, dma((NX * NYL,)), dma((PIECES,)),
            ],
            compiler_params=pltpu.CompilerParams(
                collective_id=0, has_side_effects=True, vmem_limit_bytes=60 * 1024 * 1024
            ),
            cost_estimate=pl.CostEstimate(flops=2_000_000_000, bytes_accessed=6_000_000, transcendentals=0),
        )(activations, cotangent, momentum, rows)
        return pl.pallas_call(
            close,
            out_shape=(
                jax.ShapeDtypeStruct((1, ROWS, COLS), b16),
                jax.ShapeDtypeStruct((ROWS, COLS), f32),
            ),
            in_specs=[pl.BlockSpec(memory_space=pltpu.VMEM)] * 2 + [pl.BlockSpec(memory_space=pl.ANY)],
            out_specs=(pl.BlockSpec(memory_space=pl.ANY),) * 2,
            scratch_shapes=[pltpu.VMEM((ROWS, COLS), f32), pltpu.VMEM((1, ROWS, COLS), b16), dma((NCHUNK + 1,))],
            compiler_params=pltpu.CompilerParams(vmem_limit_bytes=60 * 1024 * 1024),
            cost_estimate=pl.CostEstimate(flops=500_000_000, bytes_accessed=4_000_000, transcendentals=0),
        )(bands, rows, value)

    in_specs = (P("replica", "fsdp", None),) * 3
    out_specs = (P("replica", "fsdp", None), P("fsdp", None))
    return jax.shard_map(local, mesh=mesh, in_specs=in_specs, out_specs=out_specs, check_vma=False)
```

```python
import functools

import jax
import jax.numpy as jnp
import numpy as np
from jax import lax
from jax.experimental import pallas as pl
from jax.experimental.pallas import tpu as pltpu
from jax.sharding import PartitionSpec as P

MESH = pl.DeviceIdType.MESH
SPAN = 64
BAND = 8
DECAY = 0.9
EPS = 1e-06

T = 144
ROWS = 640
COLS = 512
NX, NYL, NZ, NH = 4, 2, 16, 4
N_REPLICA = NX * NYL * NZ
CHUNK = 128
CUT = 16
EARLY = 4
NCHUNK = ROWS // CHUNK
PIECES = 3
PACKED = 16 * PIECES
HIGH = lax.Precision.HIGHEST


def basis_table():
    freq = np.arange(BAND)[:, None]
    place = np.arange(SPAN)[None, :]
    scale = np.where(freq == 0, np.sqrt(1.0 / SPAN), np.sqrt(2.0 / SPAN))
    basis = scale * np.cos(np.pi * (2.0 * place + 1.0) * freq / (2.0 * SPAN))
    table = np.zeros((CHUNK, 128), np.float64)
    for i in range(CHUNK // SPAN):
        table[i * SPAN : (i + 1) * SPAN, i * BAND : (i + 1) * BAND] = basis.T
    return table.astype(np.float32)


def split(value):
    high = value.astype(jnp.bfloat16)
    return high, (value - high.astype(jnp.float32)).astype(jnp.bfloat16)


def turn(value, by):
    return value if by == 0 else pltpu.roll(value, by, 1)


def dot(a, b, ca, cb, precision=None):
    return lax.dot_general(
        a, b, (((ca,), (cb,)), ((), ())), preferred_element_type=jnp.float32, precision=precision
    )


def kernel(
    act, cot, mom, table,
    out_next, out_bands,
    act_v, buf_s, buf_g, cots, mom_v, tab, tab2, project, side_v, p_v, s_out, s_in, acc, next_v,
    vec, xbuf, mine, zbuf, ybuf, fin, fin_in,
    go_sem, column_sem, load_sem, sem_s, sem_g, sem_c, send_sem, fwd_sem, s_send, s_recv, out_sem,
    x_send, x_recv, z_send, z_recv, y_send, y_recv, f_send, f_recv,
):
    rep = lax.axis_index("replica")
    f = lax.axis_index("fsdp")
    x = rep // (NYL * NZ)
    yl = lax.rem(rep // NZ, NYL)
    z = lax.rem(rep, NZ)
    h = f // 2
    c = lax.rem(f, 2)
    oc = 1 - c
    s = 1 - 2 * c

    def ring(v):
        return lax.rem(v + NH, NH)

    def dev(hh, cc, xx=None, yy=None, zz=None):
        xx = x if xx is None else xx
        yy = yl if yy is None else yy
        zz = z if zz is None else zz
        return {"replica": (xx * NYL + yy) * NZ + zz, "fsdp": hh * 2 + cc}

    def remote(src, dst, ss, rs, to):
        return pltpu.make_async_remote_copy(src, dst, ss, rs, device_id=to, device_id_type=MESH)

    def block(hh, cc):
        start = pl.multiple_of((hh * 2 + cc) * ROWS, ROWS)
        return act.at[0, :, pl.ds(start, ROWS)]

    loads = [
        pltpu.make_async_copy(table, tab, load_sem.at[0]),
        pltpu.make_async_copy(cot.at[0], cots.at[2 + c], load_sem.at[1]),
        pltpu.make_async_copy(mom.at[0], mom_v, load_sem.at[2]),
        pltpu.make_async_copy(block(ring(h + s), c), buf_s.at[2 + c], load_sem.at[3]),
        pltpu.make_async_copy(block(h, c), buf_g.at[c], load_sem.at[4]),
    ]
    loads += [
        pltpu.make_async_copy(act.at[0, :, pl.ds(d * ROWS, ROWS)], act_v.at[d], load_sem.at[5 + d])
        for d in range(2 * NH)
    ]
    for copy in loads:
        copy.start()

    y = NYL * h + yl
    ny = NYL * NH
    place = lax.rem(y - NYL * x + ny, ny)

    def lead_at(where):
        where = lax.rem(where + 2 * ny, ny)
        return jnp.where(jnp.logical_and(where >= 1, where <= 5), 1, 0)

    lead_core = lead_at(place)
    leads = c == lead_core
    barrier = pltpu.get_barrier_semaphore()

    def signal(sem, to):
        pl.semaphore_signal(sem, inc=1, device_id=to, device_id_type=MESH)

    @pl.when(jnp.logical_not(leads))
    def _():
        signal(barrier, dev(h, lead_core))

    for k in (-1, 1):
        signal(barrier, dev(ring(h + k), lead_at(place + NYL * k)))
    for k in range(1, NX):
        xx = lax.rem(x + k, NX)
        signal(barrier, dev(h, lead_at(y - NYL * xx), xx=xx))

    loads[0].wait()
    rows = tab[...]
    for k in range(NCHUNK):
        high, low = split(turn(rows, 2 * BAND * k))
        tab2[k * CHUNK : (k + 1) * CHUNK] = jnp.concatenate([high, low], axis=1)
    high, low = split(dot(rows, rows, 1, 1, HIGH))
    project[...] = jnp.concatenate([high, low], axis=1)

    tells = jnp.logical_and(place == 4, c == 0)
    owns = jnp.logical_and(jnp.logical_not(leads), jnp.logical_or(place < 4, place > 5))
    piece = jnp.where(c == 0, place - 1, lax.rem(ny - place, ny))

    @pl.when(leads)
    def _():
        pl.semaphore_wait(barrier, 1 + 4 + 2 * (NX - 1))
        signal(go_sem, dev(h, 1 - lead_core))
        signal(barrier, dev(ring(x + 2), 0, yy=0))

    @pl.when(jnp.logical_not(leads))
    def _():
        pl.semaphore_wait(go_sem, 1)

    def via(core, low, high, sem):
        start = pl.multiple_of((ring(h + 2) * 2 + core) * ROWS, ROWS)
        part = act.at[0, pl.ds(low, high - low), pl.ds(start, ROWS)]
        to = dev(ring(h + 1 - 2 * core), core)
        return remote(part, buf_s.at[c, pl.ds(low, high - low)], send_sem.at[sem], sem_s.at[c], to)

    first = [
        remote(cot.at[0], cots.at[c], send_sem.at[0], sem_c.at[c], dev(ring(h + s), c)),
        remote(cot.at[0], cots.at[4 + c], send_sem.at[1], sem_c.at[4 + c], dev(ring(h - s), c)),
        remote(cot.at[0], cots.at[2 + c], send_sem.at[2], sem_c.at[2 + c], dev(h, oc)),
        remote(block(ring(h + s * -1), oc), buf_s.at[2 + c], send_sem.at[3], sem_s.at[2 + c], dev(h, oc)),
        via(0, 0, CUT, 4),
        via(1, 0, CUT, 5),
    ]
    second = [
        via(0, CUT, T, 9),
        via(1, CUT, T, 10),
        remote(block(h, oc), buf_g.at[c], send_sem.at[6], sem_g.at[c], dev(h, oc)),
        remote(block(ring(h - 1), 0), buf_g.at[2 + c], send_sem.at[7], sem_g.at[2 + c], dev(ring(h - 1), 0)),
        remote(block(ring(h + 1), 1), buf_g.at[2 + c], send_sem.at[8], sem_g.at[2 + c], dev(ring(h + 1), 1)),
    ]
    for copy in first + second[2:3]:
        copy.start()

    @pl.when(owns)
    def _():
        def greet(k, carry):
            signal(barrier, dev(h, c, zz=lax.rem(z + k, NZ)))
            return carry

        lax.fori_loop(1, NZ, greet, 0)

    for copy in loads[1:3] + loads[5:]:
        copy.wait()
    columns = tab2[0:COLS]

    def sides(value):
        high, low = split(value)
        wide = dot(high, columns, 1, 0)
        return wide[:, :128] + wide[:, 128:] + dot(low, columns[:, :128], 1, 0)

    def pack(band):
        return jnp.concatenate([band[0:40] + pltpu.roll(band[40:80], 64, 1), jnp.zeros((8, 128), jnp.float32)], axis=0)

    q = dot(cots[2 + c], columns, 1, 0)
    q = q[:, :128] + q[:, 128:]
    q_high, q_low = split(q)
    q_both = (q_high.astype(jnp.float32) + pltpu.roll(q_low.astype(jnp.float32), 64, 1)).astype(jnp.bfloat16)
    q_all = jnp.concatenate([q_both, q_high], axis=0)
    p = dot(act_v[...].reshape(2 * NH * T, ROWS), tab2[...], 1, 0)
    p = p[:, :128] + p[:, 128:]
    for d in range(2 * NH):
        p_high, p_low = split(p[d * T : (d + 1) * T])
        p_v[0:T, d * 128 : (d + 1) * 128] = p_high
        p_v[T : 2 * T, d * 128 : (d + 1) * 128] = p_low
    bands = dot(q_all, p_v[...], 0, 0)
    bands = bands[0:64] + bands[64:128]
    for d in range(2 * NH):
        part = bands[:, d * 128 : (d + 1) * 128]
        vec[d] = pack(jnp.concatenate([part, jnp.zeros_like(part)], axis=0).T)
    side_v[...] = sides(DECAY * mom_v[...])
    side_high, side_low = split(side_v[...])
    own = dot(tab2[...], side_high, 0, 0)
    own = own[0:128] + own[128:256] + dot(tab2[:, :128], side_low, 0, 0)
    vec[f] += pack(own)

    forwards = [
        remote(cots.at[c], cots.at[4 + c], fwd_sem.at[0], sem_c.at[4 + c], dev(h, oc)),
        remote(cots.at[4 + c], cots.at[c], fwd_sem.at[1], sem_c.at[c], dev(h, oc)),
    ]

    def owner_y(xx, k):
        return lax.rem(NYL * xx + jnp.where(c == 0, 1 + k, ny - k), ny)

    def y_copy(k):
        yy = owner_y(x, k)
        return remote(mine.at[pl.ds(16 * k, 16)], ybuf.at[y], y_send.at[k], y_recv, dev(yy // NYL, c, yy=lax.rem(yy, NYL)))

    def z_copy(k):
        return remote(zbuf.at[z], zbuf.at[z], z_send.at[k], z_recv, dev(h, c, zz=lax.rem(z + k, NZ)))

    f_targets = []
    for xx in range(NX):
        for yy in range(NYL):
            here = jnp.logical_and(x == xx, jnp.logical_and(h == x, yl == yy))
            f_targets.append((xx * NYL + yy, dev(x, c, xx=xx, yy=yy), here))

    def f_copy(k, there):
        return remote(fin.at[piece], fin_in.at[piece], f_send.at[k], f_recv.at[piece], there)

    def s_copy(k):
        at = pl.ds(pl.multiple_of(k * CHUNK, CHUNK), CHUNK)
        return remote(s_out.at[at], s_in.at[at], s_send.at[k], s_recv.at[k], dev(ring(h + s), c))

    def low_part(side):
        high, low = split(side)
        rows = []
        for k in range(NCHUNK):
            top = high[k * CHUNK : (k + 1) * CHUNK]
            both = jnp.concatenate([top, top], axis=0)
            rows.append(dot(project[...], both, 1, 0) + dot(project[:, :128], low[k * CHUNK : (k + 1) * CHUNK], 1, 0))
        high, low = split(jnp.concatenate(rows, axis=0))
        return dot(jnp.concatenate([high, high], axis=1), columns, 1, 1) + dot(low, columns[:, :128], 1, 1)

    def plane_copies():
        copies = [remote(vec.at[2 * x + oc], xbuf.at[c], x_send.at[0], x_recv.at[c], dev(h, oc))]
        for k in range(1, NX):
            xx = lax.rem(x + k, NX)
            for m in range(2):
                copies.append(
                    remote(vec.at[2 * xx + m], xbuf.at[2 * k + c], x_send.at[2 * k + m], x_recv.at[2 * k + c], dev(h, m, xx=xx))
                )
        return copies

    def plane_sums():
        copies = plane_copies()

        @pl.when(tells)
        def _():
            pl.semaphore_wait(barrier, ny)
            for k in range(ny):
                for m in range(2):
                    if (k, m) != (0, 0):
                        signal(column_sem, dev(ring(h + k // NYL), m, yy=k % NYL))

        def arrived(slot):
            pltpu.make_async_copy(xbuf.at[slot], xbuf.at[slot], x_recv.at[slot]).wait()

        arrived(oc)
        for slot in range(2, 2 * NX):
            arrived(slot)
        total = vec[2 * x + c] + xbuf[oc]
        for slot in range(2, 2 * NX):
            total = total + xbuf[slot]
        mine[...] = total

        @pl.when(jnp.logical_not(tells))
        def _():
            pl.semaphore_wait(column_sem, 1)

        for k in range(PIECES):
            copy = y_copy(k)
            here = owner_y(x, k) == y

            @pl.when(here)
            def _():
                ybuf[y] = mine[pl.ds(16 * k, 16)]

            @pl.when(jnp.logical_not(here))
            def _():
                copy.start()

        for copy in copies:
            copy.wait_send()

    def depth_sums():
        @pl.when(owns)
        def _():
            pl.semaphore_wait(barrier, NZ - 1)
            pltpu.make_async_copy(ybuf.at[pl.ds(0, ny - 1)], ybuf.at[pl.ds(0, ny - 1)], y_recv).wait()
            total = ybuf[0]
            for k in range(1, ny):
                total = total + ybuf[k]
            zbuf[z] = total

            for k in sorted(range(1, NZ), key=lambda k: abs(k - NZ // 2)):
                z_copy(k).start()

    def passed_on():
        loads[3].wait()
        remote(block(h, oc), buf_s.at[2 + oc], send_sem.at[3], sem_s.at[2 + oc], dev(h, oc)).wait_recv()
        for slot in range(2):
            remote(block(h, 0), buf_s.at[slot], send_sem.at[4], sem_s.at[slot], dev(h, oc)).wait_recv()
        remote(cot.at[0], cots.at[2 + oc], send_sem.at[2], sem_c.at[2 + oc], dev(h, oc)).wait_recv()
        remote(cot.at[0], cots.at[oc], send_sem.at[2], sem_c.at[oc], dev(h, oc)).wait_recv()
        remote(cot.at[0], cots.at[4 + oc], send_sem.at[2], sem_c.at[4 + oc], dev(h, oc)).wait_recv()

        acc[...] = dot(buf_s[...].reshape(4 * T, ROWS), cots[0:4].reshape(4 * T, COLS), 0, 0)
        s_out[...] = (acc[...] - low_part(sides(acc[...]))).astype(jnp.bfloat16)
        for k in range(NCHUNK):
            s_copy(k).start()

    def spread_sums():
        for k in range(PIECES):

            @pl.when(owner_y(x, k) != y)
            def _():
                y_copy(k).wait_send()

        @pl.when(owns)
        def _():
            pltpu.make_async_copy(zbuf.at[pl.ds(0, NZ - 1)], zbuf.at[pl.ds(0, NZ - 1)], z_recv).wait()
            total = zbuf[0]
            for k in range(1, NZ):
                total = total + zbuf[k]
            fin[piece] = total
            for k, there, here in f_targets:
                copy = f_copy(k, there)

                @pl.when(jnp.logical_not(here))
                def _():
                    copy.start()

            def end(k, carry):
                z_copy(k).wait_send()
                return carry

            lax.fori_loop(1, NZ, end, 0)
            for k, there, here in f_targets:
                copy = f_copy(k, there)

                @pl.when(jnp.logical_not(here))
                def _():
                    copy.wait_send()

    def direct():
        loads[4].wait()
        remote(block(h, oc), buf_g.at[oc], send_sem.at[6], sem_g.at[oc], dev(h, oc)).wait_recv()
        for slot in range(2, 4):
            remote(block(h, 0), buf_g.at[slot], send_sem.at[6], sem_g.at[slot], dev(h, oc)).wait_recv()

        acc[...] = dot(buf_g[...].reshape(4 * T, ROWS), cots[2:6].reshape(4 * T, COLS), 0, 0)
        acc[...] = DECAY * mom_v[...] + acc[...] - low_part(side_v[...] + sides(acc[...]))

    def bands_out():
        for k in range(PIECES):
            here = jnp.logical_and(h == x, owner_y(h, k) == y)

            @pl.when(jnp.logical_not(here))
            def _():
                pltpu.make_async_copy(fin_in.at[k], fin_in.at[k], f_recv.at[k]).wait()

            @pl.when(here)
            def _():
                fin_in[k] = fin[k]

        bands_copy = pltpu.make_async_copy(fin_in, out_bands, out_sem.at[NCHUNK])
        bands_copy.start()
        bands_copy.wait()

    def bulk():
        for copy in second[:2] + second[3:]:
            copy.start()

    def hand_on():
        first[0].wait_recv()
        forwards[0].start()
        first[1].wait_recv()
        forwards[1].start()

    for copy in plane_copies():
        copy.start()
    early = z < EARLY

    @pl.when(early)
    def _():
        bulk()
        hand_on()
        plane_sums()
        passed_on()
        depth_sums()

    @pl.when(jnp.logical_not(early))
    def _():
        plane_sums()
        bulk()
        hand_on()
        depth_sums()
        passed_on()

    spread_sums()
    direct()

    def out_copy(k):
        at = pl.ds(pl.multiple_of(k * CHUNK, CHUNK), CHUNK)
        return pltpu.make_async_copy(next_v.at[at], out_next.at[0, at], out_sem.at[k])

    def finish(k, carry):
        at = pl.ds(pl.multiple_of(k * CHUNK, CHUNK), CHUNK)
        s_copy(k).wait_recv()
        next_v[at] = (acc[at] + s_in[at].astype(jnp.float32)).astype(jnp.bfloat16)
        out_copy(k).start()
        return carry

    lax.fori_loop(0, NCHUNK, finish, 0)
    bands_out()

    def drain(k, carry):
        s_copy(k).wait_send()
        out_copy(k).wait()
        return carry

    lax.fori_loop(0, NCHUNK, drain, 0)
    for copy in first + second + forwards:
        copy.wait_send()


def close(bands, table, value, out_next, out_update, bands_v, table_v, update_v, value_v, sem):
    given = [
        pltpu.make_async_copy(bands, bands_v, sem.at[NCHUNK + 1]),
        pltpu.make_async_copy(table, table_v, sem.at[NCHUNK + 2]),
        pltpu.make_async_copy(value, value_v, sem.at[NCHUNK]),
    ]
    for each in given:
        each.start()
    given[0].wait()
    total = bands_v[...].reshape(PACKED, 128)[0:40] * (1.0 / N_REPLICA)
    left = lax.broadcasted_iota(jnp.int32, (40, 128), 1) < 64
    upper = jnp.where(left, total, 0.0)
    lower = jnp.where(left, pltpu.roll(total, 64, 1), 0.0)
    shared = jnp.concatenate([upper, lower, jnp.zeros((48, 128), jnp.float32)], axis=0)
    row = lax.broadcasted_iota(jnp.int32, (128, 128), 0) // BAND
    col = lax.broadcasted_iota(jnp.int32, (128, 128), 1) // BAND
    same = (row == col).astype(jnp.float32)
    same = same.astype(jnp.bfloat16)

    def both(value):
        return jnp.concatenate(split(value), axis=1)

    power = dot(same, both(shared * shared), 1, 0)
    power = dot(both(power[:, :128] + power[:, 128:]), jnp.concatenate([same, same], axis=0), 1, 0)
    shared = shared / jnp.sqrt(power * (1.0 / (SPAN * SPAN)) + EPS)
    given[2].wait()
    copy = pltpu.make_async_copy(value_v, out_next, sem.at[NCHUNK])
    copy.start()
    given[1].wait()
    rows = table_v[...]
    columns = [split(turn(rows, 2 * BAND * k)) for k in range(COLS // CHUNK)]
    high, low = split(shared)
    left, right = jnp.concatenate([high, high], axis=1), low
    wide = [
        dot(left, jnp.concatenate([a, b], axis=1), 1, 1) + dot(right, a, 1, 1) for a, b in columns
    ]
    high, low = split(jnp.concatenate(wide, axis=1))
    below = jnp.concatenate([high, low], axis=0)
    copies = []
    for k in range(NCHUNK):
        at = pl.ds(k * CHUNK, CHUNK)
        a, b = split(turn(rows, 2 * BAND * k))
        update_v[at] = dot(jnp.concatenate([a, a], axis=1), below, 1, 0) + dot(b, high, 1, 0)
        copies.append(pltpu.make_async_copy(update_v.at[at], out_update.at[at], sem.at[k]))
        copies[-1].start()
    for each in copies:
        each.wait()
    copy.wait()


def solution(mesh):
    assert mesh.shape["replica"] == N_REPLICA and mesh.shape["fsdp"] == 2 * NH
    table = basis_table()
    f32, b16, dma = jnp.float32, jnp.bfloat16, pltpu.SemaphoreType.DMA

    def local(activations, cotangent, momentum):
        rows = jnp.asarray(table)
        value, bands = pl.pallas_call(
            kernel,
            out_shape=(
                jax.ShapeDtypeStruct((1, ROWS, COLS), b16),
                jax.ShapeDtypeStruct((PIECES, 16, 128), f32),
            ),
            in_specs=[pl.BlockSpec(memory_space=pl.ANY)] * 4,
            out_specs=(pl.BlockSpec(memory_space=pl.ANY),) * 2,
            scratch_shapes=[
                pltpu.VMEM((2 * NH, T, ROWS), b16),
                pltpu.VMEM((4, T, ROWS), b16),
                pltpu.VMEM((4, T, ROWS), b16),
                pltpu.VMEM((6, T, COLS), b16),
                pltpu.VMEM((ROWS, COLS), f32),
                pltpu.VMEM((CHUNK, 128), f32),
                pltpu.VMEM((ROWS, 256), b16),
                pltpu.VMEM((CHUNK, 256), b16),
                pltpu.VMEM((ROWS, 128), f32),
                pltpu.VMEM((2 * T, 2 * NH * 128), b16),
                pltpu.VMEM((ROWS, COLS), b16),
                pltpu.VMEM((ROWS, COLS), b16),
                pltpu.VMEM((ROWS, COLS), f32),
                pltpu.VMEM((ROWS, COLS), b16),
                pltpu.VMEM((2 * NH, PACKED, 128), f32),
                pltpu.VMEM((2 * NX, PACKED, 128), f32),
                pltpu.VMEM((PACKED, 128), f32),
                pltpu.VMEM((NZ, 16, 128), f32),
                pltpu.VMEM((NH * NYL, 16, 128), f32),
                pltpu.VMEM((PIECES, 16, 128), f32),
                pltpu.VMEM((PIECES, 16, 128), f32),
                pltpu.SemaphoreType.REGULAR, pltpu.SemaphoreType.REGULAR,
                dma((5 + 2 * NH,)), dma((4,)), dma((4,)), dma((6,)), dma((11,)), dma((2,)),
                dma((NCHUNK,)), dma((NCHUNK,)), dma((NCHUNK + 1,)),
                dma((2 * NX,)), dma((2 * NX,)),
                dma((NZ,)), dma, dma((PIECES,)), dma, dma((NX * NYL,)), dma((PIECES,)),
            ],
            compiler_params=pltpu.CompilerParams(
                collective_id=0, has_side_effects=True, vmem_limit_bytes=60 * 1024 * 1024
            ),
            cost_estimate=pl.CostEstimate(flops=2_000_000_000, bytes_accessed=6_000_000, transcendentals=0),
        )(activations, cotangent, momentum, rows)
        return pl.pallas_call(
            close,
            out_shape=(
                jax.ShapeDtypeStruct((1, ROWS, COLS), b16),
                jax.ShapeDtypeStruct((ROWS, COLS), f32),
            ),
            in_specs=[pl.BlockSpec(memory_space=pl.ANY)] * 3,
            out_specs=(pl.BlockSpec(memory_space=pl.ANY),) * 2,
            scratch_shapes=[
                pltpu.VMEM((PIECES, 16, 128), f32),
                pltpu.VMEM((CHUNK, 128), f32),
                pltpu.VMEM((ROWS, COLS), f32),
                pltpu.VMEM((1, ROWS, COLS), b16),
                dma((NCHUNK + 3,)),
            ],
            compiler_params=pltpu.CompilerParams(vmem_limit_bytes=60 * 1024 * 1024),
            cost_estimate=pl.CostEstimate(flops=500_000_000, bytes_accessed=4_000_000, transcendentals=0),
        )(bands, rows, value)

    in_specs = (P("replica", "fsdp", None),) * 3
    out_specs = (P("replica", "fsdp", None), P("fsdp", None))
    return jax.shard_map(local, mesh=mesh, in_specs=in_specs, out_specs=out_specs, check_vma=False)
```

```python
import functools

import jax
import jax.numpy as jnp
import numpy as np
from jax import lax
from jax.experimental import pallas as pl
from jax.experimental.pallas import tpu as pltpu
from jax.sharding import PartitionSpec as P

MESH = pl.DeviceIdType.MESH
SPAN = 64
BAND = 8
DECAY = 0.9
EPS = 1e-06

T = 144
ROWS = 640
COLS = 512
NX, NYL, NZ, NH = 4, 2, 16, 4
N_REPLICA = NX * NYL * NZ
CHUNK = 128
CUT = 16
EARLY = 4
NCHUNK = ROWS // CHUNK
PIECES = 3
PACKED = 16 * PIECES
HIGH = lax.Precision.HIGHEST


def basis_table():
    freq = np.arange(BAND)[:, None]
    place = np.arange(SPAN)[None, :]
    scale = np.where(freq == 0, np.sqrt(1.0 / SPAN), np.sqrt(2.0 / SPAN))
    basis = scale * np.cos(np.pi * (2.0 * place + 1.0) * freq / (2.0 * SPAN))
    table = np.zeros((CHUNK, 128), np.float64)
    for i in range(CHUNK // SPAN):
        table[i * SPAN : (i + 1) * SPAN, i * BAND : (i + 1) * BAND] = basis.T
    return table.astype(np.float32)


def split(value):
    high = value.astype(jnp.bfloat16)
    return high, (value - high.astype(jnp.float32)).astype(jnp.bfloat16)


def turn(value, by):
    return value if by == 0 else pltpu.roll(value, by, 1)


def dot(a, b, ca, cb, precision=None):
    return lax.dot_general(
        a, b, (((ca,), (cb,)), ((), ())), preferred_element_type=jnp.float32, precision=precision
    )


def kernel(
    act, cot, mom, table,
    out_next, out_bands,
    act_v, buf_s, buf_g, cots, mom_v, tab, tab2, project, side_v, p_v, s_out, s_in, acc, next_v,
    vec, xbuf, mine, zbuf, ybuf, fin, fin_in,
    go_sem, column_sem, load_sem, sem_s, sem_g, sem_c, send_sem, fwd_sem, s_send, s_recv, out_sem,
    x_send, x_recv, z_send, z_recv, y_send, y_recv, f_send, f_recv,
):
    rep = lax.axis_index("replica")
    f = lax.axis_index("fsdp")
    x = rep // (NYL * NZ)
    yl = lax.rem(rep // NZ, NYL)
    z = lax.rem(rep, NZ)
    h = f // 2
    c = lax.rem(f, 2)
    oc = 1 - c
    s = 1 - 2 * c

    def ring(v):
        return lax.rem(v + NH, NH)

    def dev(hh, cc, xx=None, yy=None, zz=None):
        xx = x if xx is None else xx
        yy = yl if yy is None else yy
        zz = z if zz is None else zz
        return {"replica": (xx * NYL + yy) * NZ + zz, "fsdp": hh * 2 + cc}

    def remote(src, dst, ss, rs, to):
        return pltpu.make_async_remote_copy(src, dst, ss, rs, device_id=to, device_id_type=MESH)

    def block(hh, cc):
        start = pl.multiple_of((hh * 2 + cc) * ROWS, ROWS)
        return act.at[0, :, pl.ds(start, ROWS)]

    y = NYL * h + yl
    ny = NYL * NH
    place = lax.rem(y - NYL * x + ny, ny)

    def lead_at(where):
        where = lax.rem(where + 2 * ny, ny)
        return jnp.where(jnp.logical_and(where >= 1, where <= 5), 1, 0)

    lead_core = lead_at(place)
    leads = c == lead_core
    barrier = pltpu.get_barrier_semaphore()

    def signal(sem, to):
        pl.semaphore_signal(sem, inc=1, device_id=to, device_id_type=MESH)

    @pl.when(jnp.logical_not(leads))
    def _():
        signal(barrier, dev(h, lead_core))

    for k in (-1, 1):
        signal(barrier, dev(ring(h + k), lead_at(place + NYL * k)))
    for k in range(1, NX):
        xx = lax.rem(x + k, NX)
        signal(barrier, dev(h, lead_at(y - NYL * xx), xx=xx))

    loads = [
        pltpu.make_async_copy(table, tab, load_sem.at[0]),
        pltpu.make_async_copy(cot.at[0], cots.at[2 + c], load_sem.at[1]),
        pltpu.make_async_copy(mom.at[0], mom_v, load_sem.at[2]),
        pltpu.make_async_copy(block(ring(h + s), c), buf_s.at[2 + c], load_sem.at[3]),
        pltpu.make_async_copy(block(h, c), buf_g.at[c], load_sem.at[4]),
    ]
    loads += [
        pltpu.make_async_copy(act.at[0, :, pl.ds(d * ROWS, ROWS)], act_v.at[d], load_sem.at[5 + d])
        for d in range(2 * NH)
    ]
    for copy in loads:
        copy.start()

    tells = jnp.logical_and(place == 4, c == 0)
    owns = jnp.logical_and(jnp.logical_not(leads), jnp.logical_or(place < 4, place > 5))
    piece = jnp.where(c == 0, place - 1, lax.rem(ny - place, ny))

    @pl.when(leads)
    def _():
        pl.semaphore_wait(barrier, 1 + 4 + 2 * (NX - 1))
        signal(go_sem, dev(h, 1 - lead_core))
        signal(barrier, dev(ring(x + 2), 0, yy=0))

    @pl.when(jnp.logical_not(leads))
    def _():
        pl.semaphore_wait(go_sem, 1)

    def via(core, low, high, sem):
        start = pl.multiple_of((ring(h + 2) * 2 + core) * ROWS, ROWS)
        part = act.at[0, pl.ds(low, high - low), pl.ds(start, ROWS)]
        to = dev(ring(h + 1 - 2 * core), core)
        return remote(part, buf_s.at[c, pl.ds(low, high - low)], send_sem.at[sem], sem_s.at[c], to)

    first = [
        remote(cot.at[0], cots.at[c], send_sem.at[0], sem_c.at[c], dev(ring(h + s), c)),
        remote(cot.at[0], cots.at[4 + c], send_sem.at[1], sem_c.at[4 + c], dev(ring(h - s), c)),
        remote(cot.at[0], cots.at[2 + c], send_sem.at[2], sem_c.at[2 + c], dev(h, oc)),
        remote(block(ring(h + s * -1), oc), buf_s.at[2 + c], send_sem.at[3], sem_s.at[2 + c], dev(h, oc)),
        via(0, 0, CUT, 4),
        via(1, 0, CUT, 5),
    ]
    second = [
        via(0, CUT, T, 9),
        via(1, CUT, T, 10),
        remote(block(h, oc), buf_g.at[c], send_sem.at[6], sem_g.at[c], dev(h, oc)),
        remote(block(ring(h - 1), 0), buf_g.at[2 + c], send_sem.at[7], sem_g.at[2 + c], dev(ring(h - 1), 0)),
        remote(block(ring(h + 1), 1), buf_g.at[2 + c], send_sem.at[8], sem_g.at[2 + c], dev(ring(h + 1), 1)),
    ]
    for copy in first + second[2:3]:
        copy.start()

    @pl.when(owns)
    def _():
        def greet(k, carry):
            signal(barrier, dev(h, c, zz=lax.rem(z + k, NZ)))
            return carry

        lax.fori_loop(1, NZ, greet, 0)

    loads[0].wait()
    rows = tab[...]
    for k in range(NCHUNK):
        high, low = split(turn(rows, 2 * BAND * k))
        tab2[k * CHUNK : (k + 1) * CHUNK] = jnp.concatenate([high, low], axis=1)
    high, low = split(dot(rows, rows, 1, 1, HIGH))
    project[...] = jnp.concatenate([high, low], axis=1)

    for copy in loads[1:3] + loads[5:]:
        copy.wait()
    columns = tab2[0:COLS]

    def sides(value):
        high, low = split(value)
        wide = dot(high, columns, 1, 0)
        return wide[:, :128] + wide[:, 128:] + dot(low, columns[:, :128], 1, 0)

    def pack(band):
        return jnp.concatenate([band[0:40] + pltpu.roll(band[40:80], 64, 1), jnp.zeros((8, 128), jnp.float32)], axis=0)

    q = dot(cots[2 + c], columns, 1, 0)
    q = q[:, :128] + q[:, 128:]
    q_high, q_low = split(q)
    q_both = (q_high.astype(jnp.float32) + pltpu.roll(q_low.astype(jnp.float32), 64, 1)).astype(jnp.bfloat16)
    q_all = jnp.concatenate([q_both, q_high], axis=0)
    p = dot(act_v[...].reshape(2 * NH * T, ROWS), tab2[...], 1, 0)
    p = p[:, :128] + p[:, 128:]
    for d in range(2 * NH):
        p_high, p_low = split(p[d * T : (d + 1) * T])
        p_v[0:T, d * 128 : (d + 1) * 128] = p_high
        p_v[T : 2 * T, d * 128 : (d + 1) * 128] = p_low
    bands = dot(q_all, p_v[...], 0, 0)
    bands = bands[0:64] + bands[64:128]
    for d in range(2 * NH):
        part = bands[:, d * 128 : (d + 1) * 128]
        vec[d] = pack(jnp.concatenate([part, jnp.zeros_like(part)], axis=0).T)
    side_v[...] = sides(DECAY * mom_v[...])
    side_high, side_low = split(side_v[...])
    own = dot(tab2[...], side_high, 0, 0)
    own = own[0:128] + own[128:256] + dot(tab2[:, :128], side_low, 0, 0)
    vec[f] += pack(own)

    forwards = [
        remote(cots.at[c], cots.at[4 + c], fwd_sem.at[0], sem_c.at[4 + c], dev(h, oc)),
        remote(cots.at[4 + c], cots.at[c], fwd_sem.at[1], sem_c.at[c], dev(h, oc)),
    ]

    def owner_y(xx, k):
        return lax.rem(NYL * xx + jnp.where(c == 0, 1 + k, ny - k), ny)

    def y_copy(k):
        yy = owner_y(x, k)
        return remote(mine.at[pl.ds(16 * k, 16)], ybuf.at[y], y_send.at[k], y_recv, dev(yy // NYL, c, yy=lax.rem(yy, NYL)))

    def z_copy(k):
        return remote(zbuf.at[z], zbuf.at[z], z_send.at[k], z_recv, dev(h, c, zz=lax.rem(z + k, NZ)))

    f_targets = []
    for xx in range(NX):
        for yy in range(NYL):
            here = jnp.logical_and(x == xx, jnp.logical_and(h == x, yl == yy))
            f_targets.append((xx * NYL + yy, dev(x, c, xx=xx, yy=yy), here))

    def f_copy(k, there):
        return remote(fin.at[piece], fin_in.at[piece], f_send.at[k], f_recv.at[piece], there)

    def s_copy(k):
        at = pl.ds(pl.multiple_of(k * CHUNK, CHUNK), CHUNK)
        return remote(s_out.at[at], s_in.at[at], s_send.at[k], s_recv.at[k], dev(ring(h + s), c))

    def low_part(side):
        high, low = split(side)
        rows = []
        for k in range(NCHUNK):
            top = high[k * CHUNK : (k + 1) * CHUNK]
            both = jnp.concatenate([top, top], axis=0)
            rows.append(dot(project[...], both, 1, 0) + dot(project[:, :128], low[k * CHUNK : (k + 1) * CHUNK], 1, 0))
        high, low = split(jnp.concatenate(rows, axis=0))
        return dot(jnp.concatenate([high, high], axis=1), columns, 1, 1) + dot(low, columns[:, :128], 1, 1)

    def plane_copies():
        copies = [remote(vec.at[2 * x + oc], xbuf.at[c], x_send.at[0], x_recv.at[c], dev(h, oc))]
        for k in range(1, NX):
            xx = lax.rem(x + k, NX)
            for m in range(2):
                copies.append(
                    remote(vec.at[2 * xx + m], xbuf.at[2 * k + c], x_send.at[2 * k + m], x_recv.at[2 * k + c], dev(h, m, xx=xx))
                )
        return copies

    def plane_sums():
        copies = plane_copies()

        @pl.when(tells)
        def _():
            pl.semaphore_wait(barrier, ny)
            for k in range(ny):
                for m in range(2):
                    if (k, m) != (0, 0):
                        signal(column_sem, dev(ring(h + k // NYL), m, yy=k % NYL))

        def arrived(slot):
            pltpu.make_async_copy(xbuf.at[slot], xbuf.at[slot], x_recv.at[slot]).wait()

        arrived(oc)
        for slot in range(2, 2 * NX):
            arrived(slot)
        total = vec[2 * x + c] + xbuf[oc]
        for slot in range(2, 2 * NX):
            total = total + xbuf[slot]
        mine[...] = total

        @pl.when(jnp.logical_not(tells))
        def _():
            pl.semaphore_wait(column_sem, 1)

        for k in range(PIECES):
            copy = y_copy(k)
            here = owner_y(x, k) == y

            @pl.when(here)
            def _():
                ybuf[y] = mine[pl.ds(16 * k, 16)]

            @pl.when(jnp.logical_not(here))
            def _():
                copy.start()

        for copy in copies:
            copy.wait_send()

    def depth_sums():
        @pl.when(owns)
        def _():
            pl.semaphore_wait(barrier, NZ - 1)
            pltpu.make_async_copy(ybuf.at[pl.ds(0, ny - 1)], ybuf.at[pl.ds(0, ny - 1)], y_recv).wait()
            total = ybuf[0]
            for k in range(1, ny):
                total = total + ybuf[k]
            zbuf[z] = total

            for k in sorted(range(1, NZ), key=lambda k: abs(k - NZ // 2)):
                z_copy(k).start()

    def passed_on():
        loads[3].wait()
        remote(block(h, oc), buf_s.at[2 + oc], send_sem.at[3], sem_s.at[2 + oc], dev(h, oc)).wait_recv()
        for slot in range(2):
            remote(block(h, 0), buf_s.at[slot], send_sem.at[4], sem_s.at[slot], dev(h, oc)).wait_recv()
        remote(cot.at[0], cots.at[2 + oc], send_sem.at[2], sem_c.at[2 + oc], dev(h, oc)).wait_recv()
        remote(cot.at[0], cots.at[oc], send_sem.at[2], sem_c.at[oc], dev(h, oc)).wait_recv()
        remote(cot.at[0], cots.at[4 + oc], send_sem.at[2], sem_c.at[4 + oc], dev(h, oc)).wait_recv()

        acc[...] = dot(buf_s[...].reshape(4 * T, ROWS), cots[0:4].reshape(4 * T, COLS), 0, 0)
        s_out[...] = (acc[...] - low_part(sides(acc[...]))).astype(jnp.bfloat16)
        for k in range(NCHUNK):
            s_copy(k).start()

    def spread_sums():
        for k in range(PIECES):

            @pl.when(owner_y(x, k) != y)
            def _():
                y_copy(k).wait_send()

        @pl.when(owns)
        def _():
            pltpu.make_async_copy(zbuf.at[pl.ds(0, NZ - 1)], zbuf.at[pl.ds(0, NZ - 1)], z_recv).wait()
            total = zbuf[0]
            for k in range(1, NZ):
                total = total + zbuf[k]
            fin[piece] = total
            for k, there, here in f_targets:
                copy = f_copy(k, there)

                @pl.when(jnp.logical_not(here))
                def _():
                    copy.start()

            def end(k, carry):
                z_copy(k).wait_send()
                return carry

            lax.fori_loop(1, NZ, end, 0)
            for k, there, here in f_targets:
                copy = f_copy(k, there)

                @pl.when(jnp.logical_not(here))
                def _():
                    copy.wait_send()

    def direct():
        loads[4].wait()
        remote(block(h, oc), buf_g.at[oc], send_sem.at[6], sem_g.at[oc], dev(h, oc)).wait_recv()
        for slot in range(2, 4):
            remote(block(h, 0), buf_g.at[slot], send_sem.at[6], sem_g.at[slot], dev(h, oc)).wait_recv()

        acc[...] = dot(buf_g[...].reshape(4 * T, ROWS), cots[2:6].reshape(4 * T, COLS), 0, 0)
        acc[...] = DECAY * mom_v[...] + acc[...] - low_part(side_v[...] + sides(acc[...]))

    def bands_out():
        for k in range(PIECES):
            here = jnp.logical_and(h == x, owner_y(h, k) == y)

            @pl.when(jnp.logical_not(here))
            def _():
                pltpu.make_async_copy(fin_in.at[k], fin_in.at[k], f_recv.at[k]).wait()

            @pl.when(here)
            def _():
                fin_in[k] = fin[k]

        bands_copy = pltpu.make_async_copy(fin_in, out_bands, out_sem.at[NCHUNK])
        bands_copy.start()
        bands_copy.wait()

    def bulk():
        for copy in second[:2] + second[3:]:
            copy.start()

    def hand_on():
        first[0].wait_recv()
        forwards[0].start()
        first[1].wait_recv()
        forwards[1].start()

    for copy in plane_copies():
        copy.start()
    early = z < EARLY

    @pl.when(early)
    def _():
        bulk()
        hand_on()
        plane_sums()
        passed_on()
        depth_sums()

    @pl.when(jnp.logical_not(early))
    def _():
        plane_sums()
        bulk()
        hand_on()
        depth_sums()
        passed_on()

    spread_sums()
    direct()

    def out_copy(k):
        at = pl.ds(pl.multiple_of(k * CHUNK, CHUNK), CHUNK)
        return pltpu.make_async_copy(next_v.at[at], out_next.at[0, at], out_sem.at[k])

    def finish(k, carry):
        at = pl.ds(pl.multiple_of(k * CHUNK, CHUNK), CHUNK)
        s_copy(k).wait_recv()
        next_v[at] = (acc[at] + s_in[at].astype(jnp.float32)).astype(jnp.bfloat16)
        out_copy(k).start()
        return carry

    lax.fori_loop(0, NCHUNK, finish, 0)
    bands_out()

    def drain(k, carry):
        s_copy(k).wait_send()
        out_copy(k).wait()
        return carry

    lax.fori_loop(0, NCHUNK, drain, 0)
    for copy in first + second + forwards:
        copy.wait_send()


def close(bands, table, value, out_next, out_update, bands_v, table_v, update_v, value_v, sem):
    given = [
        pltpu.make_async_copy(bands, bands_v, sem.at[NCHUNK + 1]),
        pltpu.make_async_copy(table, table_v, sem.at[NCHUNK + 2]),
        pltpu.make_async_copy(value, value_v, sem.at[NCHUNK]),
    ]
    for each in given:
        each.start()
    given[0].wait()
    total = bands_v[...].reshape(PACKED, 128)[0:40] * (1.0 / N_REPLICA)
    left = lax.broadcasted_iota(jnp.int32, (40, 128), 1) < 64
    upper = jnp.where(left, total, 0.0)
    lower = jnp.where(left, pltpu.roll(total, 64, 1), 0.0)
    shared = jnp.concatenate([upper, lower, jnp.zeros((48, 128), jnp.float32)], axis=0)
    row = lax.broadcasted_iota(jnp.int32, (128, 128), 0) // BAND
    col = lax.broadcasted_iota(jnp.int32, (128, 128), 1) // BAND
    same = (row == col).astype(jnp.float32)
    same = same.astype(jnp.bfloat16)

    def both(value):
        return jnp.concatenate(split(value), axis=1)

    power = dot(same, both(shared * shared), 1, 0)
    power = dot(both(power[:, :128] + power[:, 128:]), jnp.concatenate([same, same], axis=0), 1, 0)
    shared = shared / jnp.sqrt(power * (1.0 / (SPAN * SPAN)) + EPS)
    given[2].wait()
    copy = pltpu.make_async_copy(value_v, out_next, sem.at[NCHUNK])
    copy.start()
    given[1].wait()
    rows = table_v[...]
    columns = [split(turn(rows, 2 * BAND * k)) for k in range(COLS // CHUNK)]
    high, low = split(shared)
    left, right = jnp.concatenate([high, high], axis=1), low
    wide = [
        dot(left, jnp.concatenate([a, b], axis=1), 1, 1) + dot(right, a, 1, 1) for a, b in columns
    ]
    high, low = split(jnp.concatenate(wide, axis=1))
    below = jnp.concatenate([high, low], axis=0)
    copies = []
    for k in range(NCHUNK):
        at = pl.ds(k * CHUNK, CHUNK)
        a, b = split(turn(rows, 2 * BAND * k))
        update_v[at] = dot(jnp.concatenate([a, a], axis=1), below, 1, 0) + dot(b, high, 1, 0)
        copies.append(pltpu.make_async_copy(update_v.at[at], out_update.at[at], sem.at[k]))
        copies[-1].start()
    for each in copies:
        each.wait()
    copy.wait()


def solution(mesh):
    assert mesh.shape["replica"] == N_REPLICA and mesh.shape["fsdp"] == 2 * NH
    table = basis_table()
    f32, b16, dma = jnp.float32, jnp.bfloat16, pltpu.SemaphoreType.DMA

    def local(activations, cotangent, momentum):
        rows = jnp.asarray(table)
        value, bands = pl.pallas_call(
            kernel,
            out_shape=(
                jax.ShapeDtypeStruct((1, ROWS, COLS), b16),
                jax.ShapeDtypeStruct((PIECES, 16, 128), f32),
            ),
            in_specs=[pl.BlockSpec(memory_space=pl.ANY)] * 4,
            out_specs=(pl.BlockSpec(memory_space=pl.ANY),) * 2,
            scratch_shapes=[
                pltpu.VMEM((2 * NH, T, ROWS), b16),
                pltpu.VMEM((4, T, ROWS), b16),
                pltpu.VMEM((4, T, ROWS), b16),
                pltpu.VMEM((6, T, COLS), b16),
                pltpu.VMEM((ROWS, COLS), f32),
                pltpu.VMEM((CHUNK, 128), f32),
                pltpu.VMEM((ROWS, 256), b16),
                pltpu.VMEM((CHUNK, 256), b16),
                pltpu.VMEM((ROWS, 128), f32),
                pltpu.VMEM((2 * T, 2 * NH * 128), b16),
                pltpu.VMEM((ROWS, COLS), b16),
                pltpu.VMEM((ROWS, COLS), b16),
                pltpu.VMEM((ROWS, COLS), f32),
                pltpu.VMEM((ROWS, COLS), b16),
                pltpu.VMEM((2 * NH, PACKED, 128), f32),
                pltpu.VMEM((2 * NX, PACKED, 128), f32),
                pltpu.VMEM((PACKED, 128), f32),
                pltpu.VMEM((NZ, 16, 128), f32),
                pltpu.VMEM((NH * NYL, 16, 128), f32),
                pltpu.VMEM((PIECES, 16, 128), f32),
                pltpu.VMEM((PIECES, 16, 128), f32),
                pltpu.SemaphoreType.REGULAR, pltpu.SemaphoreType.REGULAR,
                dma((5 + 2 * NH,)), dma((4,)), dma((4,)), dma((6,)), dma((11,)), dma((2,)),
                dma((NCHUNK,)), dma((NCHUNK,)), dma((NCHUNK + 1,)),
                dma((2 * NX,)), dma((2 * NX,)),
                dma((NZ,)), dma, dma((PIECES,)), dma, dma((NX * NYL,)), dma((PIECES,)),
            ],
            compiler_params=pltpu.CompilerParams(
                collective_id=0, has_side_effects=True, vmem_limit_bytes=60 * 1024 * 1024
            ),
            cost_estimate=pl.CostEstimate(flops=2_000_000_000, bytes_accessed=6_000_000, transcendentals=0),
        )(activations, cotangent, momentum, rows)
        return pl.pallas_call(
            close,
            out_shape=(
                jax.ShapeDtypeStruct((1, ROWS, COLS), b16),
                jax.ShapeDtypeStruct((ROWS, COLS), f32),
            ),
            in_specs=[pl.BlockSpec(memory_space=pl.ANY)] * 3,
            out_specs=(pl.BlockSpec(memory_space=pl.ANY),) * 2,
            scratch_shapes=[
                pltpu.VMEM((PIECES, 16, 128), f32),
                pltpu.VMEM((CHUNK, 128), f32),
                pltpu.VMEM((ROWS, COLS), f32),
                pltpu.VMEM((1, ROWS, COLS), b16),
                dma((NCHUNK + 3,)),
            ],
            compiler_params=pltpu.CompilerParams(vmem_limit_bytes=60 * 1024 * 1024),
            cost_estimate=pl.CostEstimate(flops=500_000_000, bytes_accessed=4_000_000, transcendentals=0),
        )(bands, rows, value)

    in_specs = (P("replica", "fsdp", None),) * 3
    out_specs = (P("replica", "fsdp", None), P("fsdp", None))
    return jax.shard_map(local, mesh=mesh, in_specs=in_specs, out_specs=out_specs, check_vma=False)
```

```python
import functools

import jax
import jax.numpy as jnp
import numpy as np
from jax import lax
from jax.experimental import pallas as pl
from jax.experimental.pallas import tpu as pltpu
from jax.sharding import PartitionSpec as P

MESH = pl.DeviceIdType.MESH
SPAN = 64
BAND = 8
DECAY = 0.9
EPS = 1e-06

T = 144
ROWS = 640
COLS = 512
NX, NYL, NZ, NH = 4, 2, 16, 4
N_REPLICA = NX * NYL * NZ
CHUNK = 128
CUT = 16
EARLY = 4
NCHUNK = ROWS // CHUNK
PIECES = 3
PACKED = 16 * PIECES
HIGH = lax.Precision.HIGHEST


def basis_table():
    freq = np.arange(BAND)[:, None]
    place = np.arange(SPAN)[None, :]
    scale = np.where(freq == 0, np.sqrt(1.0 / SPAN), np.sqrt(2.0 / SPAN))
    basis = scale * np.cos(np.pi * (2.0 * place + 1.0) * freq / (2.0 * SPAN))
    table = np.zeros((CHUNK, 128), np.float64)
    for i in range(CHUNK // SPAN):
        table[i * SPAN : (i + 1) * SPAN, i * BAND : (i + 1) * BAND] = basis.T
    return table.astype(np.float32)


def split(value):
    high = value.astype(jnp.bfloat16)
    return high, (value - high.astype(jnp.float32)).astype(jnp.bfloat16)


def turn(value, by):
    return value if by == 0 else pltpu.roll(value, by, 1)


def dot(a, b, ca, cb, precision=None):
    return lax.dot_general(
        a, b, (((ca,), (cb,)), ((), ())), preferred_element_type=jnp.float32, precision=precision
    )


def kernel(
    act, cot, mom, table,
    out_next, out_bands,
    act_v, buf_s, buf_g, cots, mom_v, tab, tab2, project, side_v, p_v, s_out, s_in, acc, next_v,
    vec, xbuf, mine, zbuf, ybuf, fin, fin_in, shared_v,
    go_sem, column_sem, load_sem, sem_s, sem_g, sem_c, send_sem, fwd_sem, s_send, s_recv, out_sem,
    x_send, x_recv, z_send, z_recv, y_send, y_recv, f_send, f_recv,
):
    rep = lax.axis_index("replica")
    f = lax.axis_index("fsdp")
    x = rep // (NYL * NZ)
    yl = lax.rem(rep // NZ, NYL)
    z = lax.rem(rep, NZ)
    h = f // 2
    c = lax.rem(f, 2)
    oc = 1 - c
    s = 1 - 2 * c

    def ring(v):
        return lax.rem(v + NH, NH)

    def dev(hh, cc, xx=None, yy=None, zz=None):
        xx = x if xx is None else xx
        yy = yl if yy is None else yy
        zz = z if zz is None else zz
        return {"replica": (xx * NYL + yy) * NZ + zz, "fsdp": hh * 2 + cc}

    def remote(src, dst, ss, rs, to):
        return pltpu.make_async_remote_copy(src, dst, ss, rs, device_id=to, device_id_type=MESH)

    def block(hh, cc):
        start = pl.multiple_of((hh * 2 + cc) * ROWS, ROWS)
        return act.at[0, :, pl.ds(start, ROWS)]

    y = NYL * h + yl
    ny = NYL * NH
    place = lax.rem(y - NYL * x + ny, ny)

    def lead_at(where):
        where = lax.rem(where + 2 * ny, ny)
        return jnp.where(jnp.logical_and(where >= 1, where <= 5), 1, 0)

    lead_core = lead_at(place)
    leads = c == lead_core
    barrier = pltpu.get_barrier_semaphore()

    def signal(sem, to):
        pl.semaphore_signal(sem, inc=1, device_id=to, device_id_type=MESH)

    @pl.when(jnp.logical_not(leads))
    def _():
        signal(barrier, dev(h, lead_core))

    for k in (-1, 1):
        signal(barrier, dev(ring(h + k), lead_at(place + NYL * k)))
    for k in range(1, NX):
        xx = lax.rem(x + k, NX)
        signal(barrier, dev(h, lead_at(y - NYL * xx), xx=xx))

    loads = [
        pltpu.make_async_copy(table, tab, load_sem.at[0]),
        pltpu.make_async_copy(cot.at[0], cots.at[2 + c], load_sem.at[1]),
        pltpu.make_async_copy(mom.at[0], mom_v, load_sem.at[2]),
        pltpu.make_async_copy(block(ring(h + s), c), buf_s.at[2 + c], load_sem.at[3]),
        pltpu.make_async_copy(block(h, c), buf_g.at[c], load_sem.at[4]),
    ]
    loads += [
        pltpu.make_async_copy(act.at[0, :, pl.ds(d * ROWS, ROWS)], act_v.at[d], load_sem.at[5 + d])
        for d in range(2 * NH)
    ]
    for copy in loads:
        copy.start()

    tells = jnp.logical_and(place == 4, c == 0)
    owns = jnp.logical_and(jnp.logical_not(leads), jnp.logical_or(place < 4, place > 5))
    piece = jnp.where(c == 0, place - 1, lax.rem(ny - place, ny))

    @pl.when(leads)
    def _():
        pl.semaphore_wait(barrier, 1 + 4 + 2 * (NX - 1))
        signal(go_sem, dev(h, 1 - lead_core))
        signal(barrier, dev(ring(x + 2), 0, yy=0))

    @pl.when(jnp.logical_not(leads))
    def _():
        pl.semaphore_wait(go_sem, 1)

    def via(core, low, high, sem):
        start = pl.multiple_of((ring(h + 2) * 2 + core) * ROWS, ROWS)
        part = act.at[0, pl.ds(low, high - low), pl.ds(start, ROWS)]
        to = dev(ring(h + 1 - 2 * core), core)
        return remote(part, buf_s.at[c, pl.ds(low, high - low)], send_sem.at[sem], sem_s.at[c], to)

    first = [
        remote(cot.at[0], cots.at[c], send_sem.at[0], sem_c.at[c], dev(ring(h + s), c)),
        remote(cot.at[0], cots.at[4 + c], send_sem.at[1], sem_c.at[4 + c], dev(ring(h - s), c)),
        remote(cot.at[0], cots.at[2 + c], send_sem.at[2], sem_c.at[2 + c], dev(h, oc)),
        remote(block(ring(h + s * -1), oc), buf_s.at[2 + c], send_sem.at[3], sem_s.at[2 + c], dev(h, oc)),
        via(0, 0, CUT, 4),
        via(1, 0, CUT, 5),
    ]
    second = [
        via(0, CUT, T, 9),
        via(1, CUT, T, 10),
        remote(block(h, oc), buf_g.at[c], send_sem.at[6], sem_g.at[c], dev(h, oc)),
        remote(block(ring(h - 1), 0), buf_g.at[2 + c], send_sem.at[7], sem_g.at[2 + c], dev(ring(h - 1), 0)),
        remote(block(ring(h + 1), 1), buf_g.at[2 + c], send_sem.at[8], sem_g.at[2 + c], dev(ring(h + 1), 1)),
    ]
    for copy in first + second[2:3]:
        copy.start()

    @pl.when(owns)
    def _():
        def greet(k, carry):
            signal(barrier, dev(h, c, zz=lax.rem(z + k, NZ)))
            return carry

        lax.fori_loop(1, NZ, greet, 0)

    loads[0].wait()
    rows = tab[...]
    for k in range(NCHUNK):
        high, low = split(turn(rows, 2 * BAND * k))
        tab2[k * CHUNK : (k + 1) * CHUNK] = jnp.concatenate([high, low], axis=1)
    high, low = split(dot(rows, rows, 1, 1, HIGH))
    project[...] = jnp.concatenate([high, low], axis=1)

    for copy in loads[1:3] + loads[5:]:
        copy.wait()
    columns = tab2[0:COLS]

    def sides(value):
        high, low = split(value)
        wide = dot(high, columns, 1, 0)
        return wide[:, :128] + wide[:, 128:] + dot(low, columns[:, :128], 1, 0)

    def pack(band):
        return jnp.concatenate([band[0:40] + pltpu.roll(band[40:80], 64, 1), jnp.zeros((8, 128), jnp.float32)], axis=0)

    q = dot(cots[2 + c], columns, 1, 0)
    q = q[:, :128] + q[:, 128:]
    q_high, q_low = split(q)
    q_both = (q_high.astype(jnp.float32) + pltpu.roll(q_low.astype(jnp.float32), 64, 1)).astype(jnp.bfloat16)
    q_all = jnp.concatenate([q_both, q_high], axis=0)
    p = dot(act_v[...].reshape(2 * NH * T, ROWS), tab2[...], 1, 0)
    p = p[:, :128] + p[:, 128:]
    for d in range(2 * NH):
        p_high, p_low = split(p[d * T : (d + 1) * T])
        p_v[0:T, d * 128 : (d + 1) * 128] = p_high
        p_v[T : 2 * T, d * 128 : (d + 1) * 128] = p_low
    bands = dot(q_all, p_v[...], 0, 0)
    bands = bands[0:64] + bands[64:128]
    for d in range(2 * NH):
        part = bands[:, d * 128 : (d + 1) * 128]
        vec[d] = pack(jnp.concatenate([part, jnp.zeros_like(part)], axis=0).T)
    side_v[...] = sides(DECAY * mom_v[...])
    side_high, side_low = split(side_v[...])
    own = dot(tab2[...], side_high, 0, 0)
    own = own[0:128] + own[128:256] + dot(tab2[:, :128], side_low, 0, 0)
    vec[f] += pack(own)

    forwards = [
        remote(cots.at[c], cots.at[4 + c], fwd_sem.at[0], sem_c.at[4 + c], dev(h, oc)),
        remote(cots.at[4 + c], cots.at[c], fwd_sem.at[1], sem_c.at[c], dev(h, oc)),
    ]

    def owner_y(xx, k):
        return lax.rem(NYL * xx + jnp.where(c == 0, 1 + k, ny - k), ny)

    def y_copy(k):
        yy = owner_y(x, k)
        return remote(mine.at[pl.ds(16 * k, 16)], ybuf.at[y], y_send.at[k], y_recv, dev(yy // NYL, c, yy=lax.rem(yy, NYL)))

    def z_copy(k):
        return remote(zbuf.at[z], zbuf.at[z], z_send.at[k], z_recv, dev(h, c, zz=lax.rem(z + k, NZ)))

    f_targets = []
    for xx in range(NX):
        for yy in range(NYL):
            here = jnp.logical_and(x == xx, jnp.logical_and(h == x, yl == yy))
            f_targets.append((xx * NYL + yy, dev(x, c, xx=xx, yy=yy), here))

    def f_copy(k, there):
        return remote(fin.at[piece], fin_in.at[piece], f_send.at[k], f_recv.at[piece], there)

    def s_copy(k):
        at = pl.ds(pl.multiple_of(k * CHUNK, CHUNK), CHUNK)
        return remote(s_out.at[at], s_in.at[at], s_send.at[k], s_recv.at[k], dev(ring(h + s), c))

    def low_part(side):
        high, low = split(side)
        rows = []
        for k in range(NCHUNK):
            top = high[k * CHUNK : (k + 1) * CHUNK]
            both = jnp.concatenate([top, top], axis=0)
            rows.append(dot(project[...], both, 1, 0) + dot(project[:, :128], low[k * CHUNK : (k + 1) * CHUNK], 1, 0))
        high, low = split(jnp.concatenate(rows, axis=0))
        return dot(jnp.concatenate([high, high], axis=1), columns, 1, 1) + dot(low, columns[:, :128], 1, 1)

    def plane_copies():
        copies = [remote(vec.at[2 * x + oc], xbuf.at[c], x_send.at[0], x_recv.at[c], dev(h, oc))]
        for k in range(1, NX):
            xx = lax.rem(x + k, NX)
            for m in range(2):
                copies.append(
                    remote(vec.at[2 * xx + m], xbuf.at[2 * k + c], x_send.at[2 * k + m], x_recv.at[2 * k + c], dev(h, m, xx=xx))
                )
        return copies

    def plane_sums():
        copies = plane_copies()

        @pl.when(tells)
        def _():
            pl.semaphore_wait(barrier, ny)
            for k in range(ny):
                for m in range(2):
                    if (k, m) != (0, 0):
                        signal(column_sem, dev(ring(h + k // NYL), m, yy=k % NYL))

        def arrived(slot):
            pltpu.make_async_copy(xbuf.at[slot], xbuf.at[slot], x_recv.at[slot]).wait()

        arrived(oc)
        for slot in range(2, 2 * NX):
            arrived(slot)
        total = vec[2 * x + c] + xbuf[oc]
        for slot in range(2, 2 * NX):
            total = total + xbuf[slot]
        mine[...] = total

        @pl.when(jnp.logical_not(tells))
        def _():
            pl.semaphore_wait(column_sem, 1)

        for k in range(PIECES):
            copy = y_copy(k)
            here = owner_y(x, k) == y

            @pl.when(here)
            def _():
                ybuf[y] = mine[pl.ds(16 * k, 16)]

            @pl.when(jnp.logical_not(here))
            def _():
                copy.start()

        for copy in copies:
            copy.wait_send()

    def depth_sums():
        @pl.when(owns)
        def _():
            pl.semaphore_wait(barrier, NZ - 1)
            pltpu.make_async_copy(ybuf.at[pl.ds(0, ny - 1)], ybuf.at[pl.ds(0, ny - 1)], y_recv).wait()
            total = ybuf[0]
            for k in range(1, ny):
                total = total + ybuf[k]
            zbuf[z] = total

            for k in sorted(range(1, NZ), key=lambda k: abs(k - NZ // 2)):
                z_copy(k).start()

    def passed_on():
        loads[3].wait()
        remote(block(h, oc), buf_s.at[2 + oc], send_sem.at[3], sem_s.at[2 + oc], dev(h, oc)).wait_recv()
        for slot in range(2):
            remote(block(h, 0), buf_s.at[slot], send_sem.at[4], sem_s.at[slot], dev(h, oc)).wait_recv()
        remote(cot.at[0], cots.at[2 + oc], send_sem.at[2], sem_c.at[2 + oc], dev(h, oc)).wait_recv()
        remote(cot.at[0], cots.at[oc], send_sem.at[2], sem_c.at[oc], dev(h, oc)).wait_recv()
        remote(cot.at[0], cots.at[4 + oc], send_sem.at[2], sem_c.at[4 + oc], dev(h, oc)).wait_recv()

        acc[...] = dot(buf_s[...].reshape(4 * T, ROWS), cots[0:4].reshape(4 * T, COLS), 0, 0)
        s_out[...] = (acc[...] - low_part(sides(acc[...]))).astype(jnp.bfloat16)
        for k in range(NCHUNK):
            s_copy(k).start()

    def spread_sums():
        for k in range(PIECES):

            @pl.when(owner_y(x, k) != y)
            def _():
                y_copy(k).wait_send()

        @pl.when(owns)
        def _():
            pltpu.make_async_copy(zbuf.at[pl.ds(0, NZ - 1)], zbuf.at[pl.ds(0, NZ - 1)], z_recv).wait()
            total = zbuf[0]
            for k in range(1, NZ):
                total = total + zbuf[k]
            fin[piece] = total
            for k, there, here in f_targets:
                copy = f_copy(k, there)

                @pl.when(jnp.logical_not(here))
                def _():
                    copy.start()

            def end(k, carry):
                z_copy(k).wait_send()
                return carry

            lax.fori_loop(1, NZ, end, 0)
            for k, there, here in f_targets:
                copy = f_copy(k, there)

                @pl.when(jnp.logical_not(here))
                def _():
                    copy.wait_send()

    def direct():
        loads[4].wait()
        remote(block(h, oc), buf_g.at[oc], send_sem.at[6], sem_g.at[oc], dev(h, oc)).wait_recv()
        for slot in range(2, 4):
            remote(block(h, 0), buf_g.at[slot], send_sem.at[6], sem_g.at[slot], dev(h, oc)).wait_recv()

        acc[...] = dot(buf_g[...].reshape(4 * T, ROWS), cots[2:6].reshape(4 * T, COLS), 0, 0)
        acc[...] = DECAY * mom_v[...] + acc[...] - low_part(side_v[...] + sides(acc[...]))

    bands_copy = pltpu.make_async_copy(shared_v, out_bands, out_sem.at[NCHUNK])

    def bands_out():
        for k in range(PIECES):
            here = jnp.logical_and(h == x, owner_y(h, k) == y)

            @pl.when(jnp.logical_not(here))
            def _():
                pltpu.make_async_copy(fin_in.at[k], fin_in.at[k], f_recv.at[k]).wait()

            @pl.when(here)
            def _():
                fin_in[k] = fin[k]

        total = fin_in[...].reshape(PACKED, 128)[0:40] * (1.0 / N_REPLICA)
        left = lax.broadcasted_iota(jnp.int32, (40, 128), 1) < 64
        upper = jnp.where(left, total, 0.0)
        lower = jnp.where(left, pltpu.roll(total, 64, 1), 0.0)
        shared = jnp.concatenate([upper, lower, jnp.zeros((48, 128), jnp.float32)], axis=0)
        row = lax.broadcasted_iota(jnp.int32, (128, 128), 0) // BAND
        col = lax.broadcasted_iota(jnp.int32, (128, 128), 1) // BAND
        same = (row == col).astype(jnp.float32)
        same = same.astype(jnp.bfloat16)

        def both(value):
            return jnp.concatenate(split(value), axis=1)

        power = dot(same, both(shared * shared), 1, 0)
        power = dot(both(power[:, :128] + power[:, 128:]), jnp.concatenate([same, same], axis=0), 1, 0)
        shared_v[...] = shared / jnp.sqrt(power * (1.0 / (SPAN * SPAN)) + EPS)
        bands_copy.start()

    def bulk():
        for copy in second[:2] + second[3:]:
            copy.start()

    def hand_on():
        first[0].wait_recv()
        forwards[0].start()
        first[1].wait_recv()
        forwards[1].start()

    for copy in plane_copies():
        copy.start()
    early = z < EARLY

    @pl.when(early)
    def _():
        bulk()
        hand_on()
        plane_sums()
        passed_on()
        depth_sums()

    @pl.when(jnp.logical_not(early))
    def _():
        plane_sums()
        bulk()
        hand_on()
        depth_sums()
        passed_on()

    spread_sums()
    direct()

    def out_copy(k):
        at = pl.ds(pl.multiple_of(k * CHUNK, CHUNK), CHUNK)
        return pltpu.make_async_copy(next_v.at[at], out_next.at[0, at], out_sem.at[k])

    def finish(k, carry):
        at = pl.ds(pl.multiple_of(k * CHUNK, CHUNK), CHUNK)
        s_copy(k).wait_recv()
        next_v[at] = (acc[at] + s_in[at].astype(jnp.float32)).astype(jnp.bfloat16)
        out_copy(k).start()
        return carry

    pl.when(jnp.logical_not(early))(bands_out)
    lax.fori_loop(0, NCHUNK, finish, 0)
    pl.when(early)(bands_out)

    def drain(k, carry):
        s_copy(k).wait_send()
        out_copy(k).wait()
        return carry

    lax.fori_loop(0, NCHUNK, drain, 0)
    bands_copy.wait()
    for copy in first + second + forwards:
        copy.wait_send()


def close(bands, table, value, out_next, out_update, bands_v, table_v, update_v, value_v, sem):
    given = [
        pltpu.make_async_copy(bands, bands_v, sem.at[NCHUNK + 1]),
        pltpu.make_async_copy(table, table_v, sem.at[NCHUNK + 2]),
        pltpu.make_async_copy(value, value_v, sem.at[NCHUNK]),
    ]
    for each in given:
        each.start()
    given[0].wait()
    shared = bands_v[...]
    given[2].wait()
    copy = pltpu.make_async_copy(value_v, out_next, sem.at[NCHUNK])
    copy.start()
    given[1].wait()
    rows = table_v[...]
    columns = [split(turn(rows, 2 * BAND * k)) for k in range(COLS // CHUNK)]
    high, low = split(shared)
    left, right = jnp.concatenate([high, high], axis=1), low
    wide = [
        dot(left, jnp.concatenate([a, b], axis=1), 1, 1) + dot(right, a, 1, 1) for a, b in columns
    ]
    high, low = split(jnp.concatenate(wide, axis=1))
    below = jnp.concatenate([high, low], axis=0)
    copies = []
    for k in range(NCHUNK):
        at = pl.ds(k * CHUNK, CHUNK)
        a, b = split(turn(rows, 2 * BAND * k))
        update_v[at] = dot(jnp.concatenate([a, a], axis=1), below, 1, 0) + dot(b, high, 1, 0)
        copies.append(pltpu.make_async_copy(update_v.at[at], out_update.at[at], sem.at[k]))
        copies[-1].start()
    for each in copies:
        each.wait()
    copy.wait()


def solution(mesh):
    assert mesh.shape["replica"] == N_REPLICA and mesh.shape["fsdp"] == 2 * NH
    table = basis_table()
    f32, b16, dma = jnp.float32, jnp.bfloat16, pltpu.SemaphoreType.DMA

    def local(activations, cotangent, momentum):
        rows = jnp.asarray(table)
        value, bands = pl.pallas_call(
            kernel,
            out_shape=(
                jax.ShapeDtypeStruct((1, ROWS, COLS), b16),
                jax.ShapeDtypeStruct((128, 128), f32),
            ),
            in_specs=[pl.BlockSpec(memory_space=pl.ANY)] * 4,
            out_specs=(pl.BlockSpec(memory_space=pl.ANY),) * 2,
            scratch_shapes=[
                pltpu.VMEM((2 * NH, T, ROWS), b16),
                pltpu.VMEM((4, T, ROWS), b16),
                pltpu.VMEM((4, T, ROWS), b16),
                pltpu.VMEM((6, T, COLS), b16),
                pltpu.VMEM((ROWS, COLS), f32),
                pltpu.VMEM((CHUNK, 128), f32),
                pltpu.VMEM((ROWS, 256), b16),
                pltpu.VMEM((CHUNK, 256), b16),
                pltpu.VMEM((ROWS, 128), f32),
                pltpu.VMEM((2 * T, 2 * NH * 128), b16),
                pltpu.VMEM((ROWS, COLS), b16),
                pltpu.VMEM((ROWS, COLS), b16),
                pltpu.VMEM((ROWS, COLS), f32),
                pltpu.VMEM((ROWS, COLS), b16),
                pltpu.VMEM((2 * NH, PACKED, 128), f32),
                pltpu.VMEM((2 * NX, PACKED, 128), f32),
                pltpu.VMEM((PACKED, 128), f32),
                pltpu.VMEM((NZ, 16, 128), f32),
                pltpu.VMEM((NH * NYL, 16, 128), f32),
                pltpu.VMEM((PIECES, 16, 128), f32),
                pltpu.VMEM((PIECES, 16, 128), f32),
                pltpu.VMEM((128, 128), f32),
                pltpu.SemaphoreType.REGULAR, pltpu.SemaphoreType.REGULAR,
                dma((5 + 2 * NH,)), dma((4,)), dma((4,)), dma((6,)), dma((11,)), dma((2,)),
                dma((NCHUNK,)), dma((NCHUNK,)), dma((NCHUNK + 1,)),
                dma((2 * NX,)), dma((2 * NX,)),
                dma((NZ,)), dma, dma((PIECES,)), dma, dma((NX * NYL,)), dma((PIECES,)),
            ],
            compiler_params=pltpu.CompilerParams(
                collective_id=0, has_side_effects=True, vmem_limit_bytes=60 * 1024 * 1024
            ),
            cost_estimate=pl.CostEstimate(flops=2_000_000_000, bytes_accessed=6_000_000, transcendentals=0),
        )(activations, cotangent, momentum, rows)
        return pl.pallas_call(
            close,
            out_shape=(
                jax.ShapeDtypeStruct((1, ROWS, COLS), b16),
                jax.ShapeDtypeStruct((ROWS, COLS), f32),
            ),
            in_specs=[pl.BlockSpec(memory_space=pl.ANY)] * 3,
            out_specs=(pl.BlockSpec(memory_space=pl.ANY),) * 2,
            scratch_shapes=[
                pltpu.VMEM((128, 128), f32),
                pltpu.VMEM((CHUNK, 128), f32),
                pltpu.VMEM((ROWS, COLS), f32),
                pltpu.VMEM((1, ROWS, COLS), b16),
                dma((NCHUNK + 3,)),
            ],
            compiler_params=pltpu.CompilerParams(vmem_limit_bytes=60 * 1024 * 1024),
            cost_estimate=pl.CostEstimate(flops=500_000_000, bytes_accessed=4_000_000, transcendentals=0),
        )(bands, rows, value)

    in_specs = (P("replica", "fsdp", None),) * 3
    out_specs = (P("replica", "fsdp", None), P("fsdp", None))
    return jax.shard_map(local, mesh=mesh, in_specs=in_specs, out_specs=out_specs, check_vma=False)
```
